256 devices in a mesh: tm: 16 (over x, z_lo), label: 8 (over y, z_hi), vocab: 2 (over core).
Axes of the slice: x: 4, y: 4, z: 8 (z_hi: 2, z_lo: 4; z = z_hi * 4 + z_lo), core: 2. Of those that a mesh axis runs over, the one named last changes fastest.
Arguments:
- enc_rows: bfloat16 [2, 384, 640], P(None, 'tm'), may hold values from -6 to 6
- pred_rows: bfloat16 [2, 80, 640], P(None, 'label'), may hold values from -6 to 6
- enc_weight: bfloat16 [640, 640], replicated, may hold values from -0.25 to 0.25
- pred_weight: bfloat16 [640, 640], replicated, may hold values from -0.25 to 0.25
- out_weight: bfloat16 [640, 4096], P(('tm', 'label'), 'vocab'), may hold values from -0.059814453 to 0.059814453
- teacher: bfloat16 [2, 384, 80, 4096], P(None, 'tm', 'label', 'vocab'), may hold values from 9.9658966e-05 to 1
- label_ids: int32 [2, 80], P(None, 'label'), may hold values from 0 to 4095
- frame_lengths: int32 [2], replicated, may hold values from 192 to 384, as said below
- label_lengths: int32 [2], replicated, may hold values from 40 to 80, as said below
Outputs:
- pair_loss: float32 [2, 384, 80], P(None, 'tm', 'label')
- grad_enc: float32 [2, 384, 640], P(None, 'tm')
- grad_pred: float32 [2, 80, 640], P(None, 'label')
- grad_out: float32 [640, 4096], P(('tm', 'label'), 'vocab')
The draws below stay inside these ranges and needn't reach their ends.
Inputs may be any that keep to these rules, and one draw needn't show every extreme that they name: `frame_lengths`: the first utterance has all 384 frames, the others at least half of them. `label_lengths`: the first utterance has all 80 label positions, the others at least half of them.
All inputs are finite; a program needn't handle non-finite values.
Results may differ from the reference program's by a relative error of at most 0.0013.
Values may be sent and summed in bfloat16 or wider, within the bound.
A program may use at most 64 MiB of HBM per device.

```python
import math
import jax
import jax.numpy as jnp
import numpy as np
from jax import lax

E = 640
P_SIZE = 640
J = 640
V = 4096
UTTS = 2
FRAMES = 384
LABELS = 80


def draw_frame_lengths(key, part):
    key = jax.random.fold_in(key, 11)
    others = jax.random.randint(key, (UTTS - 1,), FRAMES // 2, FRAMES + 1)
    return jnp.concatenate([jnp.full((1,), FRAMES, jnp.int32), others.astype(jnp.int32)])


def draw_label_lengths(key, part):
    key = jax.random.fold_in(key, 23)
    others = jax.random.randint(key, (UTTS - 1,), LABELS // 2, LABELS + 1)
    return jnp.concatenate([jnp.full((1,), LABELS, jnp.int32), others.astype(jnp.int32)])


def touch_ends(result, rng, least, largest):
    longest = result.shape.index(max(result.shape))
    spots = []
    for shift in (0, 1):
        where = [jax.random.randint(jax.random.fold_in(rng, axis), (), 0, length) for axis, length in enumerate(result.shape)]
        where[longest] = (where[longest] + shift) % result.shape[longest]
        spots.append(tuple(where))
    return result.at[spots[0]].set(least).at[spots[1]].set(largest)


def shard_levels(key, dims, shards, least, high):
    def one(axis_at, blocks):
        heights = jax.random.uniform(jax.random.fold_in(jax.random.fold_in(key, 6), axis_at), (blocks,), jnp.float32, least / len(shards), high / len(shards))
        return jnp.repeat(jnp.exp(heights), dims[axis_at] // blocks).reshape((-1,) + (1,) * (len(dims) - axis_at - 1))

    loudness = one(*shards[0])
    for cut in shards[1:]:
        loudness = loudness * one(*cut)
    return loudness


def cumulative_ranks(count, skew):
    weights = [(1 << 20) // math.isqrt(standing ** skew) + 1 for standing in range(1, count + 1)]
    spread = 1 + sum(weights) // (1 << 30)
    return np.cumsum(np.array([max(1, weight // spread) for weight in weights]))


def skewed_ids(stream_key, extent, amount, skew):
    listing = cumulative_ranks(amount, skew)
    lot = jax.random.randint(jax.random.fold_in(stream_key, 1), extent, 0, int(listing[amount - 1]))
    rank = jnp.searchsorted(jnp.asarray(listing, jnp.int32), lot, side="right")
    return jax.random.permutation(jax.random.fold_in(stream_key, 2), amount)[rank].astype(jnp.int32)


def scatter_about(stream_key, dims, deviation, bound, pieces=(), kind=jnp.bfloat16):
    entries = deviation * jax.random.normal(stream_key, dims, jnp.float32)
    if pieces:
        entries = entries * shard_levels(stream_key, dims, pieces, -0.22, 0.18)
    return jnp.clip(entries, -bound, bound).astype(kind)


def setup_inputs(seed: int = 0) -> dict:
    keys = jax.random.split(jax.random.key(seed), 10)
    enc_rows = scatter_about(keys[0], (UTTS, FRAMES, E), 1.0, 6.0, ((1, 16),))
    pred_rows = scatter_about(keys[1], (UTTS, LABELS, P_SIZE), 1.0, 6.0, ((1, 8),))
    enc_weight = scatter_about(keys[2], (E, J), E ** -0.5, 0.25)
    pred_weight = scatter_about(keys[3], (P_SIZE, J), P_SIZE ** -0.5, 0.25)
    out_weight = jnp.clip(jax.random.uniform(keys[4], (J, V), jnp.float32, -0.059814453, 0.059814453) * shard_levels(keys[4], (J, V), ((0, 128), (1, 2)), -0.4, 0.0), -0.059814453, 0.059814453).astype(jnp.bfloat16)
    teacher = jnp.clip(jnp.exp(math.log(1.0) - 9.213757 * jax.random.uniform(keys[5], (UTTS, FRAMES, LABELS, V), jnp.float32) ** shard_levels(keys[5], (UTTS, FRAMES, LABELS, V), ((1, 16), (2, 8), (3, 2)), -0.2, 0.2)), 9.965896606445312e-05, 1.0).astype(jnp.bfloat16)
    label_ids = touch_ends(skewed_ids(keys[6], (UTTS, LABELS), V, 2), jax.random.fold_in(keys[6], 3), 0, V - 1).astype(jnp.int32)
    frame_lengths = draw_frame_lengths(jax.random.fold_in(keys[9], 71), 0)
    label_lengths = draw_label_lengths(jax.random.fold_in(keys[9], 71), 0)
    return dict(enc_rows=enc_rows, pred_rows=pred_rows, enc_weight=enc_weight, pred_weight=pred_weight, out_weight=out_weight, teacher=teacher, label_ids=label_ids, frame_lengths=frame_lengths, label_lengths=label_lengths)


label_weight = 0.5


def utterance(enc_proj, pred_proj, teacher_b, hot_b, frame_ok, label_ok, out_weight, weight_grad):
    def step(carry, items):
        weight_acc, pred_acc = carry
        enc_t, teacher_t, ok_t = items
        act = jnp.tanh(enc_t[None, :] + pred_proj)
        hidden = act.astype(jnp.bfloat16)
        logits = jnp.dot(hidden, out_weight, preferred_element_type=jnp.float32)
        post = teacher_t.astype(jnp.float32)
        total = jnp.sum(post, axis=1)
        expsum = jnp.sum(jnp.exp(logits), axis=1)
        entropy = jnp.sum(post * jnp.log(post), axis=1)
        cross = jnp.sum(post * logits, axis=1)
        picked = jnp.sum(hot_b * logits, axis=1)
        lse = jnp.log(expsum)
        mask = ok_t * label_ok
        loss = mask * (entropy / total - jnp.log(total) - cross / total + lse + label_weight * (lse - picked))
        student = jnp.exp(logits - lse[:, None])
        dlog = (mask[:, None] * ((student - post / total[:, None]) + label_weight * (student - hot_b))).astype(jnp.bfloat16)
        back = lax.dot_general(dlog, out_weight, (((1,), (1,)), ((), ())), preferred_element_type=jnp.float32)
        slope = back * (1.0 - act * act)
        weight_acc = weight_acc + lax.dot_general(hidden, dlog, (((0,), (0,)), ((), ())), preferred_element_type=jnp.float32)
        pred_acc = pred_acc + slope
        return (weight_acc, pred_acc), (loss, jnp.sum(slope, axis=0))

    start = (weight_grad, jnp.zeros(pred_proj.shape, jnp.float32))
    (weight_grad, pred_sum), (losses, enc_sum) = lax.scan(step, start, (enc_proj, teacher_b, frame_ok))
    return weight_grad, pred_sum, losses, enc_sum


def reference(enc_rows, pred_rows, enc_weight, pred_weight, out_weight, teacher, label_ids, frame_lengths, label_lengths):
    frames = enc_rows.shape[1]
    labels = pred_rows.shape[1]
    vocab_size = out_weight.shape[1]
    weight_grad = jnp.zeros(out_weight.shape, jnp.float32)
    losses, enc_grads, pred_grads = [], [], []
    for b in range(enc_rows.shape[0]):
        enc_proj = jnp.dot(enc_rows[b], enc_weight, preferred_element_type=jnp.float32)
        pred_proj = jnp.dot(pred_rows[b], pred_weight, preferred_element_type=jnp.float32)
        hot_b = (label_ids[b][:, None] == jnp.arange(vocab_size, dtype=jnp.int32)[None, :]).astype(jnp.float32)
        frame_ok = (jnp.arange(frames, dtype=jnp.int32) < frame_lengths[b]).astype(jnp.float32)
        label_ok = (jnp.arange(labels, dtype=jnp.int32) < label_lengths[b]).astype(jnp.float32)
        weight_grad, pred_sum, loss_b, enc_sum = utterance(enc_proj, pred_proj, teacher[b], hot_b, frame_ok, label_ok, out_weight, weight_grad)
        losses.append(loss_b)
        enc_grads.append(jnp.dot(enc_sum, enc_weight.astype(jnp.float32).T, precision=lax.Precision.HIGHEST))
        pred_grads.append(jnp.dot(pred_sum, pred_weight.astype(jnp.float32).T, precision=lax.Precision.HIGHEST))
    return jnp.stack(losses), jnp.stack(enc_grads), jnp.stack(pred_grads), weight_grad
```

```python
import functools

import jax
import jax.numpy as jnp
from jax import lax
from jax.experimental import pallas as pl
from jax.experimental.pallas import tpu as pltpu
from jax.sharding import PartitionSpec as P

MESH = pl.DeviceIdType.MESH
F32, BF16 = jnp.float32, jnp.bfloat16
label_weight = 0.5

SIZE = {"x": 4, "y": 4, "z": 8}
ORDERS = (("z", "y", "x"), ("z", "x", "y"), ("z", "y", "x"), ("z", "x", "y"), ("y", "x", "z"))
CHUNKS = len(ORDERS)
BLOCKS = 128
UTTS, FRAMES, LABELS = 2, 24, 10
ROWS = UTTS * FRAMES
PAIRS = ROWS * LABELS
PADDED = 512
JOINT = 640
VOCAB = 2048
TILES = VOCAB // 128
MAIN = ROWS * 8
SIDE = 40


def nt(a, b):
    return lax.dot_general(a, b, (((1,), (1,)), ((), ())), preferred_element_type=F32)


def nn(a, b):
    return jnp.dot(a, b, preferred_element_type=F32)


def split3(value):
    first = value.astype(BF16)
    rest = value - first.astype(F32)
    second = rest.astype(BF16)
    third = (rest - second.astype(F32)).astype(BF16)
    return first, second, third


def pair_place(p):
    tail = p - MAIN
    frame = jnp.where(p < MAIN, p >> 3, tail >> 1)
    label = jnp.where(p < MAIN, p & 7, 8 + (tail & 1))
    return frame, label, (frame >= FRAMES).astype(jnp.int32)


def kernel(
    frame_len, label_len, ids, enc_rows, pred_rows, own_weight, enc_weight_hbm, pred_weight_hbm, teacher_hbm,
    loss_out, enc_out, pred_out, grad_out,
    raw, weight, wide, hidden, hidden_t, act, post, expo, dlog, teacher, enc_weight, pred_weight, perm,
    proj, stats, stats_in, ident, mask, scale_a, scale_b, acc, term, ring_in, mid_in, last_in,
    side, side_in, pair_in, y_in, x_in, zh_in, zl_in, side_nat, grads, grads_in, result,
    local_sem, send_sem, recv_sem,
):
    tm, lab, core = lax.axis_index("tm"), lax.axis_index("label"), lax.axis_index("vocab")
    at = {"x": tm // 4, "y": lab // 2, "z": (lab % 2) * 4 + tm % 4}

    def device(axis, coordinate):
        where = dict(at)
        where[axis] = coordinate
        return (where["x"] * 4 + where["z"] % 4, where["y"] * 2 + where["z"] // 4, core)

    def around(axis, distance):
        return lax.rem(at[axis] + distance + SIZE[axis], SIZE[axis])

    sent = []

    def send(src, dst, target):
        number = len(sent)
        copy = pltpu.make_async_remote_copy(
            src_ref=src, dst_ref=dst, send_sem=send_sem.at[number], recv_sem=recv_sem.at[number],
            device_id=target, device_id_type=MESH,
        )
        copy.start()
        sent.append(copy)
        return copy

    local = []
    for number, (src, dst) in enumerate(((enc_weight_hbm, enc_weight), (pred_weight_hbm, pred_weight), (teacher_hbm, teacher))):
        copy = pltpu.make_async_copy(src, dst, local_sem.at[number])
        copy.start()
        local.append(copy)

    barrier = pltpu.get_barrier_semaphore()
    partners = [device(a, around(a, d)) for a in "xyz" for d in range(1, SIZE[a])] + [(tm, lab, 1 - core)]
    for target in partners:
        pl.semaphore_signal(barrier, inc=1, device_id=target, device_id_type=MESH)

    own = own_weight[...].astype(F32)
    for r in range(CHUNKS):
        for c in range(TILES):
            result[r, c : c + 1, :] = own[r : r + 1, c * 128 : (c + 1) * 128]

    def spot(r):
        first, middle, last = ORDERS[r]
        return (at[last] * SIZE[middle] + at[middle]) * SIZE[first] + at[first]

    for r in range(CHUNKS):
        raw[r, pl.ds(pl.multiple_of(spot(r) * 16, 16), 16), :] = result[r].astype(BF16)

    pl.semaphore_wait(barrier, len(partners))

    first_copies = []
    for r in range(CHUNKS):
        axis = ORDERS[r][0]
        block = raw.at[r, pl.ds(pl.multiple_of(spot(r) * 16, 16), 16), :]
        first_copies.append([send(block, block, device(axis, around(axis, d))) for d in range(1, SIZE[axis])])

    p = lax.broadcasted_iota(jnp.int32, (PADDED, 128), 0)
    lane = lax.broadcasted_iota(jnp.int32, (PADDED, 128), 1)
    frame, label, utt = pair_place(p)
    frame_ok = tm * FRAMES + frame - FRAMES * utt < jnp.where(utt == 1, frame_len[1], frame_len[0])
    label_ok = lab * LABELS + label < jnp.where(utt == 1, label_len[1], label_len[0])
    mask[...] = jnp.where(frame_ok & label_ok, 1.0, 0.0)[:PAIRS]
    emitted = jnp.zeros((PADDED, 128), jnp.int32)
    for k in range(LABELS):
        emitted = jnp.where(label == k, jnp.where(utt == 1, ids[1, k], ids[0, k]), emitted)
    ident[...] = (emitted - core * VOCAB)[:PAIRS]
    spread = jnp.where((lane == frame) | (lane == ROWS + 16 * utt + label), 1.0, 0.0).astype(BF16)

    j = lax.broadcasted_iota(jnp.int32, (JOINT, BLOCKS), 0)
    block_at = lax.broadcasted_iota(jnp.int32, (JOINT, BLOCKS), 1)
    for r in range(CHUNKS):
        first, middle, last = ORDERS[r]
        n1, n2 = SIZE[first], SIZE[middle]
        coords = {first: block_at % n1, middle: (block_at // n1) % n2, last: block_at // (n1 * n2)}
        natural = coords["x"] * 32 + (coords["z"] % 4) * 8 + coords["y"] * 2 + coords["z"] // 4
        perm[:, r * BLOCKS : (r + 1) * BLOCKS] = jnp.where(j == natural * CHUNKS + r, 1.0, 0.0).astype(BF16)

    second_copies = []
    for r in range(CHUNKS):
        first, middle, last = ORDERS[r]
        for copy in first_copies[r]:
            copy.wait_recv()
        rows = SIZE[first] * 16
        block = raw.at[r, pl.ds(pl.multiple_of((at[last] * SIZE[middle] + at[middle]) * rows, 16), rows), :]
        second_copies.append([send(block, block, device(middle, around(middle, d))) for d in range(1, SIZE[middle])])

    local[0].wait()
    local[1].wait()
    proj[...] = jnp.zeros_like(proj)
    for b in range(UTTS):
        proj[b * FRAMES : (b + 1) * FRAMES, :] = enc_rows[b].astype(F32)
        proj[ROWS + 16 * b : ROWS + 16 * b + LABELS, :] = pred_rows[b].astype(F32)
    proj[0:ROWS, :] = nn(proj[0:ROWS, :].astype(BF16), enc_weight[...])
    proj[ROWS : ROWS + 32, :] = nn(proj[ROWS : ROWS + 32, :].astype(BF16), pred_weight[...])
    ordered = sum(nn(part, perm[...]) for part in split3(proj[...]))
    proj[...] = ordered

    def block_of(ref, r, coordinate, half=None):
        first, middle, last = ORDERS[r]
        rows = SIZE[first] * SIZE[middle] * 16
        start = coordinate * rows
        if half is not None:
            rows //= 2
            start = start + half * rows
        return ref.at[r, pl.ds(pl.multiple_of(start, 16), rows), :]

    def ring_gather(r, step):
        axis = ORDERS[r][2]
        n = SIZE[axis]
        copies = []
        for way, half in ((1, 0), (-1, 1)):
            block = block_of(raw, r, around(axis, -way * step), half if step == n // 2 - 1 else None)
            copies.append(send(block, block, device(axis, around(axis, way))))
        return copies

    ring = {}
    for r in range(CHUNKS):
        for copy in second_copies[r]:
            copy.wait_recv()
        ring[r, 0] = ring_gather(r, 0)

    act[...] = jnp.tanh(sum(nn(spread, part) for part in split3(proj[...])))
    hidden[...] = act[...].astype(BF16)
    hidden_t[...] = act[...].T.astype(BF16)

    def ring_next(r, step):
        for copy in ring[r, step - 1]:
            copy.wait_recv()
        ring[r, step] = ring_gather(r, step)

    for r in range(CHUNKS):
        ring_next(r, 1)

    local[2].wait()
    lane8 = lax.broadcasted_iota(jnp.int32, (8, 128), 1)

    def teacher_rows(rows, start):
        post[pl.ds(pl.multiple_of(start, 8), 8), :] = rows
        total = jnp.sum(rows, axis=1, keepdims=True)
        ent = jnp.sum(rows * jnp.log(rows), axis=1, keepdims=True)
        stats[pl.ds(pl.multiple_of(start, 8), 8), :] = jnp.where(lane8 == 1, total, jnp.where(lane8 == 2, ent, 0.0))

    def teacher_step(g, carry):
        tails = []
        for k in range(4):
            rows = teacher[4 * g + k].astype(F32)
            teacher_rows(rows[0:8], 32 * g + 8 * k)
            tails.append(rows[8:10])
        teacher_rows(jnp.concatenate(tails, axis=0), MAIN + 8 * g)
        return carry

    lax.fori_loop(0, 4, teacher_step, 0)
    ring_next(4, 2)
    lax.fori_loop(4, 8, teacher_step, 0)
    ring_next(4, 3)
    lax.fori_loop(8, 12, teacher_step, 0)

    for r in range(CHUNKS):
        for copy in ring[r, SIZE[ORDERS[r][2]] // 2 - 1]:
            copy.wait_recv()
        wide[...] = raw[r].astype(F32)
        for c in range(TILES):
            weight[r * BLOCKS : (r + 1) * BLOCKS, c * 128 : (c + 1) * 128] = wide[pl.ds(c, BLOCKS, stride=16), :].astype(BF16)

    acc[...] = jnp.zeros_like(acc)
    lanes = lax.broadcasted_iota(jnp.int32, (PAIRS, 128), 1)
    width = 512
    for start in range(0, VOCAB, width):
        logits = nn(hidden[0:PAIRS, :], weight[:, start : start + width])
        powers = jnp.exp(logits)
        expo[:, start : start + width] = powers
        for c in range(0, width, 128):
            part = logits[:, c : c + 128]
            acc[0] += powers[:, c : c + 128]
            acc[1] += post[:, start + c : start + c + 128] * part
            acc[2] += jnp.where(lanes + (start + c) == ident[...], part, 0.0)
    expsum = jnp.sum(acc[0], axis=1, keepdims=True)
    cross = jnp.sum(acc[1], axis=1, keepdims=True)
    picked = jnp.sum(acc[2], axis=1, keepdims=True)
    stats[...] += jnp.where(lanes == 0, expsum, jnp.where(lanes == 3, cross, jnp.where(lanes == 4, picked, 0.0)))
    other_core = (tm, lab, 1 - core)
    stats_copy = send(stats, stats_in, other_core)
    dlog[PAIRS:PADDED, :] = jnp.zeros((PADDED - PAIRS, VOCAB), BF16)
    stats_copy.wait_recv()

    sums = stats[...] + stats_in[...]
    expsum, total, ent, cross, picked = (sums[:, k : k + 1] for k in range(5))
    scale_a[...] = (1.0 + label_weight) * mask[...] / expsum
    scale_b[...] = mask[...] / total
    lse = jnp.log(expsum)
    pair_loss = ent / total - jnp.log(total) - cross / total + lse + label_weight * (lse - picked)

    def dlog_step(g, carry):
        rows = pl.ds(pl.multiple_of(32 * g, 32), 32)
        a, b, hot, ident_g = scale_a[rows, :], scale_b[rows, :], label_weight * mask[rows, :], ident[rows, :]
        lane_g = lax.broadcasted_iota(jnp.int32, (32, 128), 1)
        for c in range(TILES):
            columns = slice(c * 128, (c + 1) * 128)
            value = a * expo[rows, columns] - b * post[rows, columns]
            dlog[rows, columns] = (value - jnp.where(lane_g + c * 128 == ident_g, hot, 0.0)).astype(BF16)
        return carry

    lax.fori_loop(0, PAIRS // 32, dlog_step, 0)

    def term_block(r, coordinate, half=None):
        return block_of(term, r, coordinate, half)

    def ring_reduce(r, step):
        axis = ORDERS[r][2]
        n = SIZE[axis]
        rows = BLOCKS * 16 // n
        copies = []
        for way, half, slot in ((1, 0, 0), (-1, 1, 1)):
            distance = n // 2 - step
            block = term_block(r, around(axis, way * distance), half if step == 0 else None)
            size = rows // 2 if step == 0 else rows
            place = ring_in.at[r, pl.ds((2 * step + slot) * rows, size), :]
            copies.append(send(block, place, device(axis, around(axis, way))))
        return copies

    def ring_add(r, step):
        axis = ORDERS[r][2]
        n = SIZE[axis]
        rows = BLOCKS * 16 // n
        for copy in ring[r, step]:
            copy.wait_recv()
        for way, half, slot in ((1, 0, 0), (-1, 1, 1)):
            distance = n // 2 - step - 1
            size = rows // 2 if step == 0 else rows
            start = around(axis, way * distance) * rows + (half * size if step == 0 else 0)
            place = pl.ds(pl.multiple_of(start, 16), size)
            base = (2 * step + slot) * rows
            term[r, place, :] += ring_in[r, base : base + size, :]

    for r in range(CHUNKS):
        product = nn(hidden_t[r * BLOCKS : (r + 1) * BLOCKS, :], dlog[...])
        for c in range(TILES):
            term[r, pl.ds(c, BLOCKS, stride=16), :] = product[:, c * 128 : (c + 1) * 128]
        ring[r, 0] = ring_reduce(r, 0)

    back = nt(dlog[...], weight[...])
    slope = back * (1.0 - act[...] * act[...])
    q = lax.broadcasted_iota(jnp.int32, (2 * SIDE, PADDED), 0)
    frame_p, label_p, utt_p = pair_place(lax.broadcasted_iota(jnp.int32, (2 * SIDE, PADDED), 1))
    utt_q = (q >= SIDE).astype(jnp.int32)
    place_q = q - SIDE * utt_q
    is_enc = (place_q < FRAMES) & (frame_p == FRAMES * utt_q + place_q)
    is_pred = (place_q >= FRAMES) & (utt_p == utt_q) & (label_p == place_q - FRAMES)
    gather_sums = jnp.where(is_enc | is_pred, 1.0, 0.0).astype(BF16)
    side[...] = sum(nn(gather_sums, part) for part in split3(slope))
    theirs = side.at[pl.ds(pl.multiple_of((1 - core) * SIDE, 8), SIDE), :]
    pair_copy = send(theirs, pair_in, other_core)

    for r in range(CHUNKS):
        ring_add(r, 0)
        ring[r, 1] = ring_reduce(r, 1)

    pair_copy.wait_recv()
    side_nat[...] = side[pl.ds(pl.multiple_of(core * SIDE, 8), SIDE), :] + pair_in[...]
    enc_part, pred_part = side_nat.at[0:FRAMES, :], side_nat.at[FRAMES:SIDE, :]
    y_copies = [send(enc_part, y_in.at[d - 1], device("y", around("y", d))) for d in range(1, 4)]
    x_copies = [send(pred_part, x_in.at[d - 1], device("x", around("x", d))) for d in range(1, 4)]

    _, label_c, _ = pair_place(lax.broadcasted_iota(jnp.int32, (PAIRS, 128), 0))
    acc[0] = jnp.where(lanes == label_c, mask[...] * pair_loss, 0.0)
    losses = jnp.concatenate([acc[0], jnp.zeros((PADDED - PAIRS, 128), F32)], axis=0)
    table = sum(nn(gather_sums, part) for part in split3(losses))
    for b in range(UTTS):
        loss_out[b] = table[SIDE * b : SIDE * b + FRAMES, 0:LABELS]

    ring_add(4, 1)
    ring[4, 2] = ring_reduce(4, 2)

    for copy in y_copies + x_copies:
        copy.wait_recv()
    side_in[0:FRAMES, :] = side_nat[0:FRAMES, :] + y_in[0] + y_in[1] + y_in[2]
    side_in[FRAMES:SIDE, :] = side_nat[FRAMES:SIDE, :] + x_in[0] + x_in[1] + x_in[2]
    z_low, z_high = at["z"] % 4, at["z"] // 4
    zh_copy = send(side_in.at[0:FRAMES, :], zh_in, device("z", around("z", 4)))
    zl_copies = [
        send(side_in.at[FRAMES:SIDE, :], zl_in.at[d - 1], device("z", z_high * 4 + (z_low + d) % 4)) for d in range(1, 4)
    ]

    ring_add(4, 2)
    ring[4, 3] = ring_reduce(4, 3)

    mid_copies = {}

    def finish_ring(r):
        first, middle, last = ORDERS[r]
        ring_add(r, SIZE[last] // 2 - 1)
        rows = SIZE[first] * 16
        mid_copies[r] = []
        for d in range(1, SIZE[middle]):
            start = (at[last] * SIZE[middle] + around(middle, d)) * rows
            block = term.at[r, pl.ds(pl.multiple_of(start, 16), rows), :]
            mid_copies[r].append(send(block, mid_in.at[r, d - 1, 0:rows, :], device(middle, around(middle, d))))

    last_copies = {}

    def finish_mid(r):
        first, middle, last = ORDERS[r]
        rows = SIZE[first] * 16
        for copy in mid_copies[r]:
            copy.wait_recv()
        start = (at[last] * SIZE[middle] + at[middle]) * rows
        place = pl.ds(pl.multiple_of(start, 16), rows)
        term[r, place, :] = term[r, place, :] + mid_in[r, 0, 0:rows, :] + mid_in[r, 1, 0:rows, :] + mid_in[r, 2, 0:rows, :]
        last_copies[r] = []
        for d in range(1, SIZE[first]):
            block = term.at[r, pl.ds(pl.multiple_of(start + around(first, d) * 16, 16), 16), :]
            last_copies[r].append(send(block, last_in.at[r, d - 1], device(first, around(first, d))))

    for r in range(CHUNKS):
        finish_ring(r)

    zh_copy.wait_recv()
    for copy in zl_copies:
        copy.wait_recv()
    side_nat_value = jnp.concatenate(
        [side_in[0:FRAMES, :] + zh_in[...], side_in[FRAMES:SIDE, :] + zl_in[0] + zl_in[1] + zl_in[2]], axis=0
    )
    natural = sum(nt(part, perm[...]) for part in split3(side_nat_value))
    grads[0:FRAMES, :] = sum(nt(part, enc_weight[...]) for part in split3(natural[0:FRAMES]))
    grads[FRAMES:SIDE, :] = sum(nt(part, pred_weight[...]) for part in split3(natural[FRAMES:SIDE]))
    grads_copy = send(grads, grads_in, other_core)

    for r in range(CHUNKS):
        finish_mid(r)

    enc_out[core] = grads[0:FRAMES, :]
    pred_out[core] = grads[FRAMES : FRAMES + LABELS, :]
    grads_copy.wait_recv()
    enc_out[1 - core] = grads_in[0:FRAMES, :]
    pred_out[1 - core] = grads_in[FRAMES : FRAMES + LABELS, :]

    for r in range(CHUNKS):
        for copy in last_copies[r]:
            copy.wait_recv()
        total_r = term[r, pl.ds(pl.multiple_of(spot(r) * 16, 16), 16), :]
        for d in range(1, SIZE[ORDERS[r][0]]):
            total_r = total_r + last_in[r, d - 1]
        result[r] = total_r
        for c in range(TILES):
            grad_out[r : r + 1, c * 128 : (c + 1) * 128] = result[r, c : c + 1, :]

    for copy in sent:
        copy.wait_send()


def per_device(
    enc_rows, pred_rows, enc_weight, pred_weight, out_weight, teacher, label_ids, frame_lengths, label_lengths
):
    vmem, smem, anywhere = (pl.BlockSpec(memory_space=s) for s in (pltpu.VMEM, pltpu.SMEM, pl.ANY))
    scratch = [
        pltpu.VMEM((CHUNKS, BLOCKS * 16, 128), BF16),
        pltpu.VMEM((JOINT, VOCAB), BF16),
        pltpu.VMEM((BLOCKS * 16, 128), F32),
        pltpu.VMEM((PADDED, JOINT), BF16),
        pltpu.VMEM((JOINT, PADDED), BF16),
        pltpu.VMEM((PADDED, JOINT), F32),
        pltpu.VMEM((PAIRS, VOCAB), F32),
        pltpu.VMEM((PAIRS, VOCAB), F32),
        pltpu.VMEM((PADDED, VOCAB), BF16),
        pltpu.VMEM((ROWS, LABELS, VOCAB), BF16),
        pltpu.VMEM((JOINT, JOINT), BF16),
        pltpu.VMEM((JOINT, JOINT), BF16),
        pltpu.VMEM((JOINT, JOINT), BF16),
        pltpu.VMEM((128, JOINT), F32),
        pltpu.VMEM((PAIRS, 128), F32),
        pltpu.VMEM((PAIRS, 128), F32),
        pltpu.VMEM((PAIRS, 128), jnp.int32),
        pltpu.VMEM((PAIRS, 128), F32),
        pltpu.VMEM((PAIRS, 128), F32),
        pltpu.VMEM((PAIRS, 128), F32),
        pltpu.VMEM((3, PAIRS, 128), F32),
        pltpu.VMEM((CHUNKS, BLOCKS * 16, 128), F32),
        pltpu.VMEM((CHUNKS, BLOCKS * 16, 128), F32),
        pltpu.VMEM((CHUNKS, 3, 128, 128), F32),
        pltpu.VMEM((CHUNKS, 7, 16, 128), F32),
        pltpu.VMEM((2 * SIDE, JOINT), F32),
        pltpu.VMEM((SIDE, JOINT), F32),
        pltpu.VMEM((SIDE, JOINT), F32),
        pltpu.VMEM((3, FRAMES, JOINT), F32),
        pltpu.VMEM((3, SIDE - FRAMES, JOINT), F32),
        pltpu.VMEM((FRAMES, JOINT), F32),
        pltpu.VMEM((3, SIDE - FRAMES, JOINT), F32),
        pltpu.VMEM((SIDE, JOINT), F32),
        pltpu.VMEM((SIDE, JOINT), F32),
        pltpu.VMEM((SIDE, JOINT), F32),
        pltpu.VMEM((CHUNKS, 16, 128), F32),
        pltpu.SemaphoreType.DMA((3,)),
        pltpu.SemaphoreType.DMA((160,)),
        pltpu.SemaphoreType.DMA((160,)),
    ]
    return pl.pallas_call(
        kernel,
        out_shape=(
            jax.ShapeDtypeStruct((UTTS, FRAMES, LABELS), F32),
            jax.ShapeDtypeStruct((UTTS, FRAMES, JOINT), F32),
            jax.ShapeDtypeStruct((UTTS, LABELS, JOINT), F32),
            jax.ShapeDtypeStruct((CHUNKS, VOCAB), F32),
        ),
        in_specs=[smem] * 3 + [vmem] * 3 + [anywhere] * 3,
        out_specs=(vmem,) * 4,
        scratch_shapes=scratch,
        compiler_params=pltpu.CompilerParams(
            collective_id=0, has_side_effects=True, vmem_limit_bytes=56 * 1024 * 1024
        ),
    )(
        frame_lengths, label_lengths, label_ids, enc_rows, pred_rows, out_weight, enc_weight, pred_weight,
        teacher.reshape(ROWS, LABELS, VOCAB),
    )


def solution(mesh):
    return jax.shard_map(
        per_device,
        mesh=mesh,
        in_specs=(
            P(None, "tm", None),
            P(None, "label", None),
            P(),
            P(),
            P(("tm", "label"), "vocab"),
            P(None, "tm", "label", "vocab"),
            P(None, "label"),
            P(),
            P(),
        ),
        out_specs=(
            P(None, "tm", "label"),
            P(None, "tm", None),
            P(None, "label", None),
            P(("tm", "label"), "vocab"),
        ),
        check_vma=False,
    )
```

```python
import functools

import jax
import jax.numpy as jnp
from jax import lax
from jax.experimental import pallas as pl
from jax.experimental.pallas import tpu as pltpu
from jax.sharding import PartitionSpec as P

MESH = pl.DeviceIdType.MESH
F32, BF16 = jnp.float32, jnp.bfloat16
label_weight = 0.5

SIZE = {"x": 4, "y": 4, "z": 8}
ORDERS = (("z", "y", "x"), ("z", "y", "x"), ("z", "x", "y"), ("z", "x", "y"), ("y", "x", "z"))
CHUNKS = len(ORDERS)
TRAVEL = (0, 2, 1, 3, 4)
SLOT = (0, 3, 1, 4, 2)
GATHER = (4, 0, 2, 1, 3)
PARTS = ((0, 2), (4,), (1, 3))
BLOCKS = 128
UTTS, FRAMES, LABELS = 2, 24, 10
ROWS = UTTS * FRAMES
PAIRS = ROWS * LABELS
PADDED = 512
JOINT = 640
VOCAB = 2048
TILES = VOCAB // 128
SIDE = 40
CODED = 7 * (256 + 16)
LEVELS = 32767.0


def distances(axis):
    n = SIZE[axis]
    return sorted(range(1, n), key=lambda d: -min(d, n - d))


def nt(a, b):
    return lax.dot_general(a, b, (((1,), (1,)), ((), ())), preferred_element_type=F32)


def nn(a, b):
    return jnp.dot(a, b, preferred_element_type=F32)


def split3(value):
    first = value.astype(BF16)
    rest = value - first.astype(F32)
    second = rest.astype(BF16)
    third = (rest - second.astype(F32)).astype(BF16)
    return first, second, third


def encode(block):
    rows = block.shape[0]
    tiles = block.reshape(rows // 16, 16, 128)
    peak = jnp.maximum(jnp.max(jnp.abs(tiles), axis=0), 1e-35)
    power = jnp.ceil(jnp.log2(peak) + 0.01)
    codes = jnp.round(tiles * (LEVELS * jnp.exp2(-power))[None]).reshape(rows, 128)
    return codes.astype(jnp.int32).astype(jnp.int16), power.astype(jnp.int32).astype(jnp.int16)


def decode(codes, power):
    rows = codes.shape[0]
    scale = jnp.exp2(power.astype(jnp.int32).astype(F32)) * (1.0 / LEVELS)
    tiles = codes.astype(jnp.int32).astype(F32).reshape(rows // 16, 16, 128)
    return (tiles * scale[None]).reshape(rows, 128)


def kernel(
    frame_len, label_len, ids, enc_rows, pred_rows, own_weight, enc_weight_hbm, pred_weight_hbm, teacher_hbm,
    loss_out, enc_out, pred_out, grad_out,
    raw, weight, wide, hidden, hidden_t, act, post, expo, dlog, teacher, enc_weight, pred_weight, perm,
    proj, stats, stats_in, term, coded, coded_in, mid_coded, mid_in, last_in,
    side, side_code, pair_in, y_in, x_in, zh_in, zl_in, side_nat, grads, grads_in, result,
    local_sem, send_sem, recv_sem,
):
    tm, lab, core = lax.axis_index("tm"), lax.axis_index("label"), lax.axis_index("vocab")
    at = {"x": tm // 4, "y": lab // 2, "z": (lab % 2) * 4 + tm % 4}

    def device(axis, coordinate):
        where = dict(at)
        where[axis] = coordinate
        return (where["x"] * 4 + where["z"] % 4, where["y"] * 2 + where["z"] // 4, core)

    def around(axis, distance):
        return lax.rem(at[axis] + distance, SIZE[axis])

    other_core = (tm, lab, 1 - core)
    sent = []

    def send(src, dst, target):
        number = len(sent)
        copy = pltpu.make_async_remote_copy(
            src_ref=src, dst_ref=dst, send_sem=send_sem.at[number], recv_sem=recv_sem.at[number],
            device_id=target, device_id_type=MESH,
        )
        copy.start()
        sent.append(copy)
        return copy

    def arrived(copies):
        for copy in copies:
            copy.wait_recv()

    barrier = pltpu.get_barrier_semaphore()
    partners = [device(a, around(a, d)) for a in "zyx" for d in distances(a)] + [other_core]
    for target in partners:
        pl.semaphore_signal(barrier, inc=1, device_id=target, device_id_type=MESH)

    local = []
    for number, (src, dst) in enumerate(((enc_weight_hbm, enc_weight), (pred_weight_hbm, pred_weight), (teacher_hbm, teacher))):
        copy = pltpu.make_async_copy(src, dst, local_sem.at[number])
        copy.start()
        local.append(copy)

    own = own_weight[...].astype(F32)
    for r in range(CHUNKS):
        for c in range(TILES):
            result[r, c : c + 1, :] = own[r : r + 1, c * 128 : (c + 1) * 128]

    def spot(r):
        first, middle, last = ORDERS[r]
        return (at[last] * SIZE[middle] + at[middle]) * SIZE[first] + at[first]

    for r in range(CHUNKS):
        raw[r, pl.ds(pl.multiple_of(spot(r) * 16, 16), 16), :] = result[r].astype(BF16)

    pl.semaphore_wait(barrier, len(partners))

    first_copies = {}
    for low, high in ((0, 2), (2, 4), (4, 5)):
        axis = ORDERS[low][0]
        block = raw.at[low:high, pl.ds(pl.multiple_of(spot(low) * 16, 16), 16), :]
        first_copies[low] = [send(block, block, device(axis, around(axis, d))) for d in distances(axis)]

    j = lax.broadcasted_iota(jnp.int32, (JOINT, BLOCKS), 0)
    block_at = lax.broadcasted_iota(jnp.int32, (JOINT, BLOCKS), 1)
    for r in range(CHUNKS):
        first, middle, last = ORDERS[r]
        n1, n2 = SIZE[first], SIZE[middle]
        coords = {first: block_at % n1, middle: (block_at // n1) % n2, last: block_at // (n1 * n2)}
        natural = coords["x"] * 32 + (coords["z"] % 4) * 8 + coords["y"] * 2 + coords["z"] // 4
        columns = slice(SLOT[r] * BLOCKS, (SLOT[r] + 1) * BLOCKS)
        perm[:, columns] = jnp.where(j == natural * CHUNKS + r, 1.0, 0.0).astype(BF16)

    second_copies = {}
    for r in GATHER:
        first, middle, last = ORDERS[r]
        if r in first_copies:
            arrived(first_copies[r])
        rows = SIZE[first] * 16
        block = raw.at[r, pl.ds(pl.multiple_of((at[last] * SIZE[middle] + at[middle]) * rows, 16), rows), :]
        second_copies[r] = [send(block, block, device(middle, around(middle, d))) for d in distances(middle)]

    local[0].wait()
    local[1].wait()
    proj[...] = jnp.zeros_like(proj)
    for b in range(UTTS):
        proj[b * FRAMES : (b + 1) * FRAMES, :] = enc_rows[b].astype(F32)
    for u in range(LABELS):
        proj[ROWS + UTTS * u : ROWS + UTTS * (u + 1), :] = pred_rows[u].astype(F32)
    proj[0:ROWS, :] = nn(proj[0:ROWS, :].astype(BF16), enc_weight[...])
    proj[ROWS : ROWS + 32, :] = nn(proj[ROWS : ROWS + 32, :].astype(BF16), pred_weight[...])
    proj[...] = sum(nn(part, perm[...]) for part in split3(proj[...]))

    def last_block(r, coordinate):
        first, middle, last = ORDERS[r]
        rows = SIZE[first] * SIZE[middle] * 16
        return pl.ds(pl.multiple_of(coordinate * rows, 16), rows)

    third_copies = {}
    for r in GATHER:
        last = ORDERS[r][2]
        arrived(second_copies[r])
        block = raw.at[r, last_block(r, at[last]), :]
        third_copies[r] = [send(block, block, device(last, around(last, d))) for d in distances(last)]

    for b in range(UTTS):
        for u in range(LABELS):
            start = (b * LABELS + u) * FRAMES
            row = ROWS + UTTS * u + b
            act[start : start + FRAMES, :] = jnp.tanh(proj[b * FRAMES : (b + 1) * FRAMES, :] + proj[row : row + 1, :])
    act[PAIRS:PADDED, :] = jnp.zeros((PADDED - PAIRS, JOINT), F32)
    hidden[...] = act[...].astype(BF16)
    hidden_t[...] = act[...].T.astype(BF16)

    local[2].wait()
    lanes = lax.broadcasted_iota(jnp.int32, (FRAMES, 128), 1)
    rows_at = lax.broadcasted_iota(jnp.int32, (FRAMES, 128), 0)

    def group(g):
        return pl.ds(pl.multiple_of(g * FRAMES, 8), FRAMES)

    def teacher_step(g, carry):
        total, ent = jnp.zeros((FRAMES, 128), F32), jnp.zeros((FRAMES, 128), F32)
        for c in range(TILES):
            part = teacher[g, :, c * 128 : (c + 1) * 128].astype(F32)
            post[group(g), c * 128 : (c + 1) * 128] = part
            total += part
            ent += part * jnp.log(part)
        total = jnp.sum(total, axis=1, keepdims=True)
        ent = jnp.sum(ent, axis=1, keepdims=True)
        stats[group(g), :] = jnp.where(lanes == 1, total, jnp.where(lanes == 2, ent, 0.0))
        return carry

    lax.fori_loop(0, UTTS * LABELS, teacher_step, 0)
    dlog[PAIRS:PADDED, :] = jnp.zeros((PADDED - PAIRS, VOCAB), BF16)

    def settle(r):
        arrived(third_copies[r])
        wide[...] = raw[r].astype(F32)
        base = SLOT[r] * BLOCKS
        for c in range(TILES):
            weight[base : base + BLOCKS, c * 128 : (c + 1) * 128] = wide[pl.ds(c, BLOCKS, stride=16), :].astype(BF16)

    done = 0
    for rows in PARTS:
        for r in rows:
            settle(r)
        depth = slice(done, done + len(rows) * BLOCKS)
        done += len(rows) * BLOCKS
        for start in range(0, VOCAB, 512):
            columns = slice(start, start + 512)
            product = nn(hidden[0:PAIRS, depth], weight[depth, columns])
            expo[:, columns] = product if depth.start == 0 else expo[:, columns] + product

    def local_id(g):
        utt = g // LABELS
        return ids[utt, g - LABELS * utt] - core * VOCAB

    def expo_step(g, carry):
        rows = group(g)
        emitted = local_id(g)
        zero = jnp.zeros((FRAMES, 128), F32)
        expsum, cross, picked = zero, zero, zero
        for c in range(TILES):
            columns = slice(c * 128, (c + 1) * 128)
            logits = expo[rows, columns]
            powers = jnp.exp(logits)
            expo[rows, columns] = powers
            expsum += powers
            cross += post[rows, columns] * logits
            picked += jnp.where(lanes == emitted - c * 128, logits, 0.0)
        expsum = jnp.sum(expsum, axis=1, keepdims=True)
        cross = jnp.sum(cross, axis=1, keepdims=True)
        picked = jnp.sum(picked, axis=1, keepdims=True)
        stats[rows, :] += jnp.where(lanes == 0, expsum, jnp.where(lanes == 3, cross, jnp.where(lanes == 4, picked, 0.0)))
        return carry

    lax.fori_loop(0, UTTS * LABELS, expo_step, 0, unroll=4)
    stats_copy = send(stats, stats_in, other_core)
    stats_copy.wait_recv()

    def valid(g):
        utt = g // LABELS
        frames, labels = jnp.where(utt == 1, frame_len[1], frame_len[0]), jnp.where(utt == 1, label_len[1], label_len[0])
        label_ok = jnp.where(lab * LABELS + g - LABELS * utt < labels, 1.0, 0.0)
        return jnp.where(tm * FRAMES + rows_at < frames, label_ok, 0.0)

    def dlog_step(pair, carry):
        scales = []
        for half in range(2):
            g = 2 * pair + half
            sums = stats[group(g), :] + stats_in[group(g), :]
            mask = valid(g)
            scales.append(
                (
                    (1.0 + label_weight) * mask / sums[:, 0:1],
                    mask / sums[:, 1:2],
                    label_weight * mask,
                    local_id(g),
                    group(g),
                )
            )
        for c in range(TILES):
            columns = slice(c * 128, (c + 1) * 128)
            parts = []
            for a, b, hot, emitted, rows in scales:
                value = a * expo[rows, columns] - b * post[rows, columns]
                parts.append(value - jnp.where(lanes == emitted - c * 128, hot, 0.0))
            dlog[pl.ds(pl.multiple_of(pair * 2 * FRAMES, 16), 2 * FRAMES), columns] = jnp.concatenate(parts, axis=0).astype(BF16)
        return carry

    lax.fori_loop(0, UTTS * LABELS // 2, dlog_step, 0, unroll=2)

    def ship(r, source, store, inbox, axis, rows, base):
        copies = []
        for d in distances(axis):
            start = base + around(axis, d) * rows
            codes, power = encode(source[r, pl.ds(pl.multiple_of(start, 16), rows), :])
            low = (d - 1) * (rows + 16)
            store[r, low : low + rows, :] = codes
            store[r, low + rows : low + rows + 16, :] = power
            place = slice(low, low + rows + 16)
            copies.append(send(store.at[r, place, :], inbox.at[r, place, :], device(axis, around(axis, d))))
        return copies

    def collect(r, copies, inbox, axis, rows, base):
        arrived(copies)
        place = pl.ds(pl.multiple_of(base + at[axis] * rows, 16), rows)
        total = term[r, place, :]
        for d in range(1, SIZE[axis]):
            low = (d - 1) * (rows + 16)
            total = total + decode(inbox[r, low : low + rows, :], inbox[r, low + rows : low + rows + 16, :])
        term[r, place, :] = total

    def sizes(r):
        first, middle, last = ORDERS[r]
        low = SIZE[first] * 16
        high = low * SIZE[middle]
        return low, high, at[last] * high, at[last] * high + at[middle] * low

    third = {}
    for r in TRAVEL:
        base = SLOT[r] * BLOCKS
        product = nn(hidden_t[base : base + BLOCKS, :], dlog[...])
        for c in range(TILES):
            term[r, pl.ds(c, BLOCKS, stride=16), :] = product[:, c * 128 : (c + 1) * 128]
        third[r] = ship(r, term, coded, coded_in, ORDERS[r][2], sizes(r)[1], 0)

    act[...] = nt(dlog[...], weight[...]) * (1.0 - act[...] * act[...])
    side[...] = jnp.zeros_like(side)
    for b in range(UTTS):
        over_labels = jnp.zeros((FRAMES, JOINT), F32)
        for u in range(LABELS):
            start = (b * LABELS + u) * FRAMES
            part = act[start : start + FRAMES, :]
            over_labels += part
            row = b * SIDE + FRAMES + u
            side[row : row + 1, :] = jnp.sum(part, axis=0, keepdims=True)
        side[b * SIDE : b * SIDE + FRAMES, :] = over_labels
    theirs = side.at[pl.ds(pl.multiple_of((1 - core) * SIDE, 8), SIDE), :]
    pair_copy = send(theirs, pair_in, other_core)

    second, first_hop = {}, {}

    def turn(r):
        low, high, start, _ = sizes(r)
        collect(r, third[r], coded_in, ORDERS[r][2], high, 0)
        second[r] = ship(r, term, mid_coded, mid_in, ORDERS[r][1], low, start)

    def finish(r):
        axis = ORDERS[r][0]
        size, _, start, place = sizes(r)
        collect(r, second[r], mid_in, ORDERS[r][1], size, start)
        first_hop[r] = []
        for d in distances(axis):
            block = term.at[r, pl.ds(pl.multiple_of(place + around(axis, d) * 16, 16), 16), :]
            first_hop[r].append(send(block, last_in.at[d - 1, r], device(axis, around(axis, d))))

    turn(TRAVEL[0])

    pair_copy.wait_recv()
    side_nat[...] = side[pl.ds(pl.multiple_of(core * SIDE, 8), SIDE), :] + pair_in[...]

    def fold(start, rows):
        strips = [side_nat[start : start + rows, k * 128 : (k + 1) * 128] for k in range(JOINT // 128)]
        if rows == FRAMES:
            strips.append(jnp.zeros((8, 128), F32))
        return jnp.concatenate(strips, axis=0)

    def code_side(slot):
        for start, rows, span, low in ((0, FRAMES, 128, 0), (FRAMES, SIDE - FRAMES, 80, 144)):
            codes, power = encode(fold(start, rows))
            side_code[slot, low : low + span, :] = codes
            side_code[slot, low + span : low + span + 16, :] = power

    def add_side(enc_ref, enc_count, pred_ref, pred_count):
        for ref, count, start, rows, span in ((enc_ref, enc_count, 0, FRAMES, 128), (pred_ref, pred_count, FRAMES, SIDE - FRAMES, 80)):
            total = decode(ref[0, 0:span, :], ref[0, span : span + 16, :])
            for d in range(1, count):
                total = total + decode(ref[d, 0:span, :], ref[d, span : span + 16, :])
            for k in range(JOINT // 128):
                side_nat[start : start + rows, k * 128 : (k + 1) * 128] += total[k * rows : (k + 1) * rows]

    code_side(0)
    enc_part, pred_part = side_code.at[0, 0:144, :], side_code.at[0, 144:240, :]
    y_copies = [send(enc_part, y_in.at[d - 1], device("y", around("y", d))) for d in distances("y")]
    x_copies = [send(pred_part, x_in.at[d - 1], device("x", around("x", d))) for d in distances("x")]

    turn(TRAVEL[1])

    for b in range(UTTS):
        for u in range(LABELS):
            g = b * LABELS + u
            rows = slice(g * FRAMES, (g + 1) * FRAMES)
            sums = stats[rows, :] + stats_in[rows, :]
            expsum, total, ent, cross, picked = (sums[:, k : k + 1] for k in range(5))
            lse = jnp.log(expsum)
            pair_loss = ent / total - jnp.log(total) - cross / total + lse + label_weight * (lse - picked)
            line = jnp.sum(jnp.where(lanes == rows_at, valid(g) * pair_loss, 0.0), axis=0, keepdims=True)
            loss_out[u, b : b + 1, :] = line[:, 0:FRAMES]

    turn(TRAVEL[2])
    turn(TRAVEL[3])
    finish(TRAVEL[0])
    finish(TRAVEL[1])

    arrived(y_copies + x_copies)
    add_side(y_in, 3, x_in, 3)
    code_side(1)
    z_low, z_high = at["z"] % 4, at["z"] // 4
    zh_copy = send(side_code.at[1, 0:144, :], zh_in.at[0], device("z", around("z", 4)))
    zl_copies = [
        send(side_code.at[1, 144:240, :], zl_in.at[d - 1], device("z", z_high * 4 + (z_low + d) % 4)) for d in range(1, 4)
    ]

    finish(TRAVEL[2])
    finish(TRAVEL[3])
    turn(TRAVEL[4])
    finish(TRAVEL[4])

    def stacked(value):
        return jnp.concatenate([part.astype(F32) for part in split3(value)], axis=0).astype(BF16)

    def unstacked(value):
        rows = value.shape[0] // 3
        return value[0:rows] + value[rows : 2 * rows] + value[2 * rows : 3 * rows]

    arrived([zh_copy] + zl_copies)
    add_side(zh_in, 1, zl_in, 3)
    natural = unstacked(nt(stacked(side_nat[...]), perm[...]))
    grads[0:FRAMES, :] = unstacked(nt(stacked(natural[0:FRAMES]), enc_weight[...]))
    grads[FRAMES:SIDE, :] = unstacked(nt(stacked(natural[FRAMES:SIDE]), pred_weight[...]))
    grads_copy = send(grads, grads_in, other_core)

    for r in TRAVEL:
        arrived(first_hop[r])
        total_r = term[r, pl.ds(pl.multiple_of(spot(r) * 16, 16), 16), :]
        for d in range(1, SIZE[ORDERS[r][0]]):
            total_r = total_r + last_in[d - 1, r]
        result[r] = total_r
        for c in range(TILES):
            grad_out[r : r + 1, c * 128 : (c + 1) * 128] = result[r, c : c + 1, :]

    grads_copy.wait_recv()
    enc_out[core] = grads[0:FRAMES, :]
    enc_out[1 - core] = grads_in[0:FRAMES, :]
    for u in range(LABELS):
        mine, other = grads[FRAMES + u : FRAMES + u + 1, :], grads_in[FRAMES + u : FRAMES + u + 1, :]
        pred_out[u, 0:1, :] = jnp.where(core == 0, mine, other)
        pred_out[u, 1:2, :] = jnp.where(core == 0, other, mine)

    for copy in sent:
        copy.wait_send()


def hand_over(*refs):
    half = len(refs) // 2
    for src, dst in zip(refs[:half], refs[half:]):
        dst[...] = src[...]


def per_device(
    enc_rows, pred_rows, enc_weight, pred_weight, out_weight, teacher, label_ids, frame_lengths, label_lengths
):
    vmem, smem, anywhere = (pl.BlockSpec(memory_space=s) for s in (pltpu.VMEM, pltpu.SMEM, pl.ANY))
    scratch = [
        pltpu.VMEM((CHUNKS, BLOCKS * 16, 128), BF16),
        pltpu.VMEM((JOINT, VOCAB), BF16),
        pltpu.VMEM((BLOCKS * 16, 128), F32),
        pltpu.VMEM((PADDED, JOINT), BF16),
        pltpu.VMEM((JOINT, PADDED), BF16),
        pltpu.VMEM((PADDED, JOINT), F32),
        pltpu.VMEM((PAIRS, VOCAB), F32),
        pltpu.VMEM((PAIRS, VOCAB), F32),
        pltpu.VMEM((PADDED, VOCAB), BF16),
        pltpu.VMEM((UTTS * LABELS, FRAMES, VOCAB), BF16),
        pltpu.VMEM((JOINT, JOINT), BF16),
        pltpu.VMEM((JOINT, JOINT), BF16),
        pltpu.VMEM((JOINT, JOINT), BF16),
        pltpu.VMEM((128, JOINT), F32),
        pltpu.VMEM((PAIRS, 128), F32),
        pltpu.VMEM((PAIRS, 128), F32),
        pltpu.VMEM((CHUNKS, BLOCKS * 16, 128), F32),
        pltpu.VMEM((CHUNKS, CODED, 128), jnp.int16),
        pltpu.VMEM((CHUNKS, CODED, 128), jnp.int16),
        pltpu.VMEM((CHUNKS, 3 * (128 + 16), 128), jnp.int16),
        pltpu.VMEM((CHUNKS, 3 * (128 + 16), 128), jnp.int16),
        pltpu.VMEM((7, CHUNKS, 16, 128), F32),
        pltpu.VMEM((2 * SIDE, JOINT), F32),
        pltpu.VMEM((2, 240, 128), jnp.int16),
        pltpu.VMEM((SIDE, JOINT), F32),
        pltpu.VMEM((3, 144, 128), jnp.int16),
        pltpu.VMEM((3, 96, 128), jnp.int16),
        pltpu.VMEM((1, 144, 128), jnp.int16),
        pltpu.VMEM((3, 96, 128), jnp.int16),
        pltpu.VMEM((SIDE, JOINT), F32),
        pltpu.VMEM((SIDE, JOINT), F32),
        pltpu.VMEM((SIDE, JOINT), F32),
        pltpu.VMEM((CHUNKS, 16, 128), F32),
        pltpu.SemaphoreType.DMA((3,)),
        pltpu.SemaphoreType.DMA((144,)),
        pltpu.SemaphoreType.DMA((144,)),
    ]
    shapes = (
        jax.ShapeDtypeStruct((LABELS, UTTS, FRAMES), F32),
        jax.ShapeDtypeStruct((UTTS, FRAMES, JOINT), F32),
        jax.ShapeDtypeStruct((LABELS, UTTS, JOINT), F32),
        jax.ShapeDtypeStruct((CHUNKS, VOCAB), F32),
    )
    results = pl.pallas_call(
        kernel,
        out_shape=shapes,
        in_specs=[smem] * 3 + [vmem] * 3 + [anywhere] * 3,
        out_specs=(vmem,) * 4,
        scratch_shapes=scratch,
        compiler_params=pltpu.CompilerParams(
            collective_id=0, has_side_effects=True, vmem_limit_bytes=56 * 1024 * 1024
        ),
    )(
        frame_lengths, label_lengths, label_ids, enc_rows, pred_rows.transpose(1, 0, 2), out_weight,
        enc_weight, pred_weight, teacher.transpose(0, 2, 1, 3).reshape(UTTS * LABELS, FRAMES, VOCAB),
    )
    loss, grad_enc, grad_pred, grad_out = pl.pallas_call(
        hand_over, out_shape=shapes, in_specs=[vmem] * 4, out_specs=(vmem,) * 4
    )(*results)
    return loss.transpose(1, 2, 0), grad_enc, grad_pred.transpose(1, 0, 2), grad_out


def solution(mesh):
    return jax.shard_map(
        per_device,
        mesh=mesh,
        in_specs=(
            P(None, "tm", None),
            P(None, "label", None),
            P(),
            P(),
            P(("tm", "label"), "vocab"),
            P(None, "tm", "label", "vocab"),
            P(None, "label"),
            P(),
            P(),
        ),
        out_specs=(
            P(None, "tm", "label"),
            P(None, "tm", None),
            P(None, "label", None),
            P(("tm", "label"), "vocab"),
        ),
        check_vma=False,
    )
```

```python
import functools

import jax
import jax.numpy as jnp
from jax import lax
from jax.experimental import pallas as pl
from jax.experimental.pallas import tpu as pltpu
from jax.sharding import PartitionSpec as P

MESH = pl.DeviceIdType.MESH
F32, BF16 = jnp.float32, jnp.bfloat16
label_weight = 0.5

SIZE = {"x": 4, "y": 4, "z": 8}
ORDERS = (("z", "y", "x"), ("z", "y", "x"), ("z", "x", "y"), ("z", "x", "y"), ("y", "x", "z"))
CHUNKS = len(ORDERS)
TRAVEL = (4, 0, 2, 1, 3)
SLOT = (0, 3, 1, 4, 2)
GATHER = (4, 0, 2, 1, 3)
PARTS = ((0, 2), (4,), (1, 3))
BLOCKS = 128
UTTS, FRAMES, LABELS = 2, 24, 10
ROWS = UTTS * FRAMES
PAIRS = ROWS * LABELS
PADDED = 512
JOINT = 640
VOCAB = 2048
TILES = VOCAB // 128
SIDE = 40
CODED = 7 * (256 + 16)
LEVELS = 32767.0


def distances(axis):
    n = SIZE[axis]
    return sorted(range(1, n), key=lambda d: -min(d, n - d))


def nt(a, b):
    return lax.dot_general(a, b, (((1,), (1,)), ((), ())), preferred_element_type=F32)


def nn(a, b):
    return jnp.dot(a, b, preferred_element_type=F32)


def split3(value):
    first = value.astype(BF16)
    rest = value - first.astype(F32)
    second = rest.astype(BF16)
    third = (rest - second.astype(F32)).astype(BF16)
    return first, second, third


def encode(block):
    rows = block.shape[0]
    tiles = block.reshape(rows // 16, 16, 128)
    peak = jnp.maximum(jnp.max(jnp.abs(tiles), axis=0), 1e-35)
    power = jnp.ceil(jnp.log2(peak) + 0.01)
    codes = jnp.round(tiles * (LEVELS * jnp.exp2(-power))[None]).reshape(rows, 128)
    return codes.astype(jnp.int32).astype(jnp.int16), power.astype(jnp.int32).astype(jnp.int16)


def decode(codes, power):
    rows = codes.shape[0]
    scale = jnp.exp2(power.astype(jnp.int32).astype(F32)) * (1.0 / LEVELS)
    tiles = codes.astype(jnp.int32).astype(F32).reshape(rows // 16, 16, 128)
    return (tiles * scale[None]).reshape(rows, 128)


def kernel(
    frame_len, label_len, ids, enc_rows_hbm, pred_rows_hbm, own_weight_hbm, enc_weight_hbm, pred_weight_hbm, teacher_hbm,
    loss_out, enc_out, pred_out, grad_out,
    enc_rows, pred_rows, own_weight, raw, weight, wide, hidden, hidden_t, act, post, expo, dlog, teacher, enc_weight, pred_weight, perm,
    proj, stats, stats_in, term, coded, coded_in, mid_coded, mid_in, last_code, last_in,
    side, side_code, pair_in, y_in, x_in, zh_in, zl_in, side_nat, grads, grads_in, result,
    local_sem, send_sem, recv_sem,
):
    tm, lab, core = lax.axis_index("tm"), lax.axis_index("label"), lax.axis_index("vocab")
    at = {"x": tm // 4, "y": lab // 2, "z": (lab % 2) * 4 + tm % 4}

    def device(axis, coordinate):
        where = dict(at)
        where[axis] = coordinate
        return (where["x"] * 4 + where["z"] % 4, where["y"] * 2 + where["z"] // 4, core)

    def around(axis, distance):
        return lax.rem(at[axis] + distance, SIZE[axis])

    other_core = (tm, lab, 1 - core)
    sent = []

    def send(src, dst, target):
        number = len(sent)
        copy = pltpu.make_async_remote_copy(
            src_ref=src, dst_ref=dst, send_sem=send_sem.at[number], recv_sem=recv_sem.at[number],
            device_id=target, device_id_type=MESH,
        )
        copy.start()
        sent.append(copy)
        return copy

    left = [0]

    def drain():
        for copy in sent[left[0] :]:
            copy.wait_send()
        left[0] = len(sent)

    def arrived(copies):
        for copy in copies:
            copy.wait_recv()

    barrier = pltpu.get_barrier_semaphore()
    partners = [device(a, around(a, d)) for a in "zyx" for d in distances(a)] + [other_core]
    for target in partners:
        pl.semaphore_signal(barrier, inc=1, device_id=target, device_id_type=MESH)

    local = []
    moves = (
        (own_weight_hbm, own_weight), (enc_rows_hbm, enc_rows), (pred_rows_hbm, pred_rows),
        (enc_weight_hbm, enc_weight), (pred_weight_hbm, pred_weight), (teacher_hbm, teacher),
    )
    for number, (src, dst) in enumerate(moves):
        copy = pltpu.make_async_copy(src, dst, local_sem.at[number])
        copy.start()
        local.append(copy)

    local[0].wait()
    own = own_weight[...].astype(F32)
    for r in range(CHUNKS):
        for c in range(TILES):
            result[r, c : c + 1, :] = own[r : r + 1, c * 128 : (c + 1) * 128]

    def spot(r):
        first, middle, last = ORDERS[r]
        return (at[last] * SIZE[middle] + at[middle]) * SIZE[first] + at[first]

    for r in range(CHUNKS):
        raw[r, pl.ds(pl.multiple_of(spot(r) * 16, 16), 16), :] = result[r].astype(BF16)

    pl.semaphore_wait(barrier, len(partners))

    first_copies = {}
    for low, high in ((0, 2), (2, 4), (4, 5)):
        axis = ORDERS[low][0]
        block = raw.at[low:high, pl.ds(pl.multiple_of(spot(low) * 16, 16), 16), :]
        first_copies[low] = [send(block, block, device(axis, around(axis, d))) for d in distances(axis)]

    j = lax.broadcasted_iota(jnp.int32, (JOINT, BLOCKS), 0)
    block_at = lax.broadcasted_iota(jnp.int32, (JOINT, BLOCKS), 1)
    for r in range(CHUNKS):
        first, middle, last = ORDERS[r]
        n1, n2 = SIZE[first], SIZE[middle]
        coords = {first: block_at % n1, middle: (block_at // n1) % n2, last: block_at // (n1 * n2)}
        natural = coords["x"] * 32 + (coords["z"] % 4) * 8 + coords["y"] * 2 + coords["z"] // 4
        columns = slice(SLOT[r] * BLOCKS, (SLOT[r] + 1) * BLOCKS)
        perm[:, columns] = jnp.where(j == natural * CHUNKS + r, 1.0, 0.0).astype(BF16)

    second_copies = {}
    for r in GATHER:
        first, middle, last = ORDERS[r]
        if r in first_copies:
            arrived(first_copies[r])
        rows = SIZE[first] * 16
        block = raw.at[r, pl.ds(pl.multiple_of((at[last] * SIZE[middle] + at[middle]) * rows, 16), rows), :]
        second_copies[r] = [send(block, block, device(middle, around(middle, d))) for d in distances(middle)]

    for copy in local[1:5]:
        copy.wait()
    proj[...] = jnp.zeros_like(proj)
    for b in range(UTTS):
        proj[b * FRAMES : (b + 1) * FRAMES, :] = enc_rows[b].astype(F32)
    for u in range(LABELS):
        proj[ROWS + UTTS * u : ROWS + UTTS * (u + 1), :] = pred_rows[u].astype(F32)
    proj[0:ROWS, :] = nn(proj[0:ROWS, :].astype(BF16), enc_weight[...])
    proj[ROWS : ROWS + 32, :] = nn(proj[ROWS : ROWS + 32, :].astype(BF16), pred_weight[...])
    proj[...] = sum(nn(part, perm[...]) for part in split3(proj[...]))

    def last_block(r, coordinate):
        first, middle, last = ORDERS[r]
        rows = SIZE[first] * SIZE[middle] * 16
        return pl.ds(pl.multiple_of(coordinate * rows, 16), rows)

    def part_block(r, coordinate, half):
        first, middle, last = ORDERS[r]
        rows = SIZE[first] * SIZE[middle] * 16
        return pl.ds(pl.multiple_of(coordinate * rows + half * (rows // 2), 16), rows // 2)

    third_copies = {}
    for r in GATHER:
        last = ORDERS[r][2]
        arrived(second_copies[r])
        block = raw.at[r, last_block(r, at[last]), :]
        third_copies[r] = {
            d: send(block, block, device(last, around(last, SIZE[last] + d))) for d in ((2, -2, 1, -1) if SIZE[last] == 8 else (1, -1))
        }

    def hand_on(r):
        last = ORDERS[r][2]
        n = SIZE[last]
        near = n // 4
        copies = third_copies[r]
        more = []
        for way, half in ((1, 0), (-1, 1)):
            copies[way * near].wait_recv()
            source = around(last, n - way * near)
            place = part_block(r, source, half)
            block = raw.at[r, place, :]
            more.append(send(block, block, device(last, around(last, n + way * near))))
            if n == 8:
                block = raw.at[r, last_block(r, source), :]
                more.append(send(block, block, device(last, around(last, n + way))))
        third_copies[r] = more + ([copies[1], copies[-1]] if n == 8 else [])

    for b in range(UTTS):
        for u in range(LABELS):
            start = (b * LABELS + u) * FRAMES
            row = ROWS + UTTS * u + b
            act[start : start + FRAMES, :] = jnp.tanh(proj[b * FRAMES : (b + 1) * FRAMES, :] + proj[row : row + 1, :])
    act[PAIRS:PADDED, :] = jnp.zeros((PADDED - PAIRS, JOINT), F32)
    hidden[...] = act[...].astype(BF16)
    hidden_t[...] = act[...].T.astype(BF16)

    local[5].wait()
    lanes = lax.broadcasted_iota(jnp.int32, (FRAMES, 128), 1)
    rows_at = lax.broadcasted_iota(jnp.int32, (FRAMES, 128), 0)

    def group(g):
        return pl.ds(pl.multiple_of(g * FRAMES, 8), FRAMES)

    def teacher_step(g, carry):
        total, ent = jnp.zeros((FRAMES, 128), F32), jnp.zeros((FRAMES, 128), F32)
        for c in range(TILES):
            part = teacher[g, :, c * 128 : (c + 1) * 128].astype(F32)
            post[group(g), c * 128 : (c + 1) * 128] = part
            total += part
            ent += part * jnp.log(part)
        total = jnp.sum(total, axis=1, keepdims=True)
        ent = jnp.sum(ent, axis=1, keepdims=True)
        stats[group(g), :] = jnp.where(lanes == 1, total, jnp.where(lanes == 2, ent, 0.0))
        return carry

    lax.fori_loop(0, 10, teacher_step, 0)
    for r in GATHER[:3]:
        hand_on(r)
    lax.fori_loop(10, UTTS * LABELS, teacher_step, 0)
    dlog[PAIRS:PADDED, :] = jnp.zeros((PADDED - PAIRS, VOCAB), BF16)
    for r in GATHER[3:]:
        hand_on(r)

    def settle(r):
        arrived(third_copies[r])
        wide[...] = raw[r].astype(F32)
        base = SLOT[r] * BLOCKS
        for c in range(TILES):
            weight[base : base + BLOCKS, c * 128 : (c + 1) * 128] = wide[pl.ds(c, BLOCKS, stride=16), :].astype(BF16)

    done = 0
    for rows in PARTS:
        for r in rows:
            settle(r)
        depth = slice(done, done + len(rows) * BLOCKS)
        done += len(rows) * BLOCKS
        for start in range(0, VOCAB, 512):
            columns = slice(start, start + 512)
            product = nn(hidden[0:PAIRS, depth], weight[depth, columns])
            expo[:, columns] = product if depth.start == 0 else expo[:, columns] + product

    def local_id(g):
        utt = g // LABELS
        return ids[utt, g - LABELS * utt] - core * VOCAB

    def expo_step(g, carry):
        rows = group(g)
        emitted = local_id(g)
        zero = jnp.zeros((FRAMES, 128), F32)
        expsum, cross, picked = zero, zero, zero
        for c in range(TILES):
            columns = slice(c * 128, (c + 1) * 128)
            logits = expo[rows, columns]
            powers = jnp.exp(logits)
            expo[rows, columns] = powers
            expsum += powers
            cross += post[rows, columns] * logits
            picked += jnp.where(lanes == emitted - c * 128, logits, 0.0)
        expsum = jnp.sum(expsum, axis=1, keepdims=True)
        cross = jnp.sum(cross, axis=1, keepdims=True)
        picked = jnp.sum(picked, axis=1, keepdims=True)
        stats[rows, :] += jnp.where(lanes == 0, expsum, jnp.where(lanes == 3, cross, jnp.where(lanes == 4, picked, 0.0)))
        return carry

    lax.fori_loop(0, UTTS * LABELS, expo_step, 0, unroll=4)
    stats_copy = send(stats, stats_in, other_core)
    stats_copy.wait_recv()

    def valid(g):
        utt = g // LABELS
        frames, labels = jnp.where(utt == 1, frame_len[1], frame_len[0]), jnp.where(utt == 1, label_len[1], label_len[0])
        label_ok = jnp.where(lab * LABELS + g - LABELS * utt < labels, 1.0, 0.0)
        return jnp.where(tm * FRAMES + rows_at < frames, label_ok, 0.0)

    def dlog_step(pair, carry):
        scales = []
        for half in range(2):
            g = 2 * pair + half
            sums = stats[group(g), :] + stats_in[group(g), :]
            mask = valid(g)
            scales.append(
                (
                    (1.0 + label_weight) * mask / sums[:, 0:1],
                    mask / sums[:, 1:2],
                    label_weight * mask,
                    local_id(g),
                    group(g),
                )
            )
        for c in range(TILES):
            columns = slice(c * 128, (c + 1) * 128)
            parts = []
            for a, b, hot, emitted, rows in scales:
                value = a * expo[rows, columns] - b * post[rows, columns]
                parts.append(value - jnp.where(lanes == emitted - c * 128, hot, 0.0))
            dlog[pl.ds(pl.multiple_of(pair * 2 * FRAMES, 16), 2 * FRAMES), columns] = jnp.concatenate(parts, axis=0).astype(BF16)
        return carry

    lax.fori_loop(0, UTTS * LABELS // 2, dlog_step, 0, unroll=2)

    def ship(r, source, store, inbox, axis, rows, base):
        copies = []
        for d in distances(axis):
            start = base + around(axis, d) * rows
            codes, power = encode(source[r, pl.ds(pl.multiple_of(start, 16), rows), :])
            low = (d - 1) * (rows + 16)
            store[r, low : low + rows, :] = codes
            store[r, low + rows : low + rows + 16, :] = power
            place = slice(low, low + rows + 16)
            copies.append(send(store.at[r, place, :], inbox.at[r, place, :], device(axis, around(axis, d))))
        return copies

    def collect(r, copies, inbox, axis, rows, base):
        arrived(copies)
        place = pl.ds(pl.multiple_of(base + at[axis] * rows, 16), rows)
        total = term[r, place, :]
        for d in range(1, SIZE[axis]):
            low = (d - 1) * (rows + 16)
            total = total + decode(inbox[r, low : low + rows, :], inbox[r, low + rows : low + rows + 16, :])
        term[r, place, :] = total

    def sizes(r):
        first, middle, last = ORDERS[r]
        low = SIZE[first] * 16
        high = low * SIZE[middle]
        return low, high, at[last] * high, at[last] * high + at[middle] * low

    gathered = len(sent)
    third = {}

    def multiply(r):
        base = SLOT[r] * BLOCKS
        product = nn(hidden_t[base : base + BLOCKS, :], dlog[...])
        for c in range(TILES):
            term[r, pl.ds(c, BLOCKS, stride=16), :] = product[:, c * 128 : (c + 1) * 128]

    def depart(r):
        third[r] = ship(r, term, coded, coded_in, ORDERS[r][2], sizes(r)[1], 0)

    for r in (4, 0, 2):
        multiply(r)
        depart(r)

    act[...] = nt(dlog[...], weight[...]) * (1.0 - act[...] * act[...])
    side[...] = jnp.zeros_like(side)
    for b in range(UTTS):
        over_labels = jnp.zeros((FRAMES, JOINT), F32)
        for u in range(LABELS):
            start = (b * LABELS + u) * FRAMES
            part = act[start : start + FRAMES, :]
            over_labels += part
            row = b * SIDE + FRAMES + u
            side[row : row + 1, :] = jnp.sum(part, axis=0, keepdims=True)
        side[b * SIDE : b * SIDE + FRAMES, :] = over_labels
    theirs = side.at[pl.ds(pl.multiple_of((1 - core) * SIDE, 8), SIDE), :]
    pair_copy = send(theirs, pair_in, other_core)

    second, first_hop = {}, {}

    def turn(r):
        low, high, start, _ = sizes(r)
        collect(r, third[r], coded_in, ORDERS[r][2], high, 0)
        second[r] = ship(r, term, mid_coded, mid_in, ORDERS[r][1], low, start)

    def finish(low, high):
        axis = ORDERS[low][0]
        size, _, start, place = sizes(low)
        for r in range(low, high):
            collect(r, second[r], mid_in, ORDERS[r][1], size, start)
        first_hop[low] = []
        rows, base = (high - low) * 16, low * 24
        for d in distances(axis):
            spot_d = pl.ds(pl.multiple_of(place + around(axis, d) * 16, 16), 16)
            codes, power = encode(jnp.concatenate([term[r, spot_d, :] for r in range(low, high)], axis=0))
            last_code[d - 1, base : base + rows, :] = codes
            last_code[d - 1, base + rows : base + rows + 16, :] = power
            block = slice(base, base + rows + 16)
            first_hop[low].append(send(last_code.at[d - 1, block, :], last_in.at[d - 1, block, :], device(axis, around(axis, d))))

    for copy in sent[:gathered]:
        copy.wait_send()
    left[0] = gathered

    multiply(1)
    pair_copy.wait_recv()
    side_nat[...] = side[pl.ds(pl.multiple_of(core * SIDE, 8), SIDE), :] + pair_in[...]

    def fold(start, rows):
        strips = [side_nat[start : start + rows, k * 128 : (k + 1) * 128] for k in range(JOINT // 128)]
        if rows == FRAMES:
            strips.append(jnp.zeros((8, 128), F32))
        return jnp.concatenate(strips, axis=0)

    def code_side(slot):
        for start, rows, span, low in ((0, FRAMES, 128, 0), (FRAMES, SIDE - FRAMES, 80, 144)):
            codes, power = encode(fold(start, rows))
            side_code[slot, low : low + span, :] = codes
            side_code[slot, low + span : low + span + 16, :] = power

    def add_side(enc_ref, enc_count, pred_ref, pred_count):
        for ref, count, start, rows, span in ((enc_ref, enc_count, 0, FRAMES, 128), (pred_ref, pred_count, FRAMES, SIDE - FRAMES, 80)):
            total = decode(ref[0, 0:span, :], ref[0, span : span + 16, :])
            for d in range(1, count):
                total = total + decode(ref[d, 0:span, :], ref[d, span : span + 16, :])
            for k in range(JOINT // 128):
                side_nat[start : start + rows, k * 128 : (k + 1) * 128] += total[k * rows : (k + 1) * rows]

    code_side(0)
    enc_part, pred_part = side_code.at[0, 0:144, :], side_code.at[0, 144:240, :]
    y_copies = [send(enc_part, y_in.at[d - 1], device("y", around("y", d))) for d in distances("y")]
    x_copies = [send(pred_part, x_in.at[d - 1], device("x", around("x", d))) for d in distances("x")]

    depart(1)
    multiply(3)
    depart(3)

    for b in range(UTTS):
        for u in range(LABELS):
            g = b * LABELS + u
            rows = slice(g * FRAMES, (g + 1) * FRAMES)
            sums = stats[rows, :] + stats_in[rows, :]
            expsum, total, ent, cross, picked = (sums[:, k : k + 1] for k in range(5))
            lse = jnp.log(expsum)
            pair_loss = ent / total - jnp.log(total) - cross / total + lse + label_weight * (lse - picked)
            line = jnp.sum(jnp.where(lanes == rows_at, valid(g) * pair_loss, 0.0), axis=0, keepdims=True)
            loss_out[u, b : b + 1, :] = line[:, 0:FRAMES]

    turn(0)
    turn(2)

    arrived(y_copies + x_copies)
    add_side(y_in, 3, x_in, 3)
    code_side(1)
    z_low, z_high = at["z"] % 4, at["z"] // 4
    zh_copy = send(side_code.at[1, 0:144, :], zh_in.at[0], device("z", around("z", 4)))
    zl_copies = [
        send(side_code.at[1, 144:240, :], zl_in.at[d - 1], device("z", z_high * 4 + (z_low + d) % 4)) for d in range(1, 4)
    ]

    turn(4)
    turn(1)
    turn(3)
    drain()
    finish(4, 5)

    finish(0, 2)
    finish(2, 4)

    def stacked(value):
        return jnp.concatenate([part.astype(F32) for part in split3(value)], axis=0).astype(BF16)

    def unstacked(value):
        rows = value.shape[0] // 3
        return value[0:rows] + value[rows : 2 * rows] + value[2 * rows : 3 * rows]

    arrived([zh_copy] + zl_copies)
    add_side(zh_in, 1, zl_in, 3)
    natural = unstacked(nt(stacked(side_nat[...]), perm[...]))
    grads[0:FRAMES, :] = unstacked(nt(stacked(natural[0:FRAMES]), enc_weight[...]))
    grads[FRAMES:SIDE, :] = unstacked(nt(stacked(natural[FRAMES:SIDE]), pred_weight[...]))
    grads_copy = send(grads, grads_in, other_core)

    drain()
    for low, high in ((4, 5), (0, 2), (2, 4)):
        arrived(first_hop[low])
        rows, base = (high - low) * 16, low * 24
        total = jnp.concatenate(
            [term[r, pl.ds(pl.multiple_of(spot(r) * 16, 16), 16), :] for r in range(low, high)], axis=0
        )
        for d in distances(ORDERS[low][0]):
            total = total + decode(last_in[d - 1, base : base + rows, :], last_in[d - 1, base + rows : base + rows + 16, :])
        for r in range(low, high):
            result[r] = total[(r - low) * 16 : (r - low + 1) * 16]
            for c in range(TILES):
                grad_out[r : r + 1, c * 128 : (c + 1) * 128] = result[r, c : c + 1, :]

    grads_copy.wait_recv()
    enc_out[core] = grads[0:FRAMES, :]
    enc_out[1 - core] = grads_in[0:FRAMES, :]
    for u in range(LABELS):
        mine, other = grads[FRAMES + u : FRAMES + u + 1, :], grads_in[FRAMES + u : FRAMES + u + 1, :]
        pred_out[u, 0:1, :] = jnp.where(core == 0, mine, other)
        pred_out[u, 1:2, :] = jnp.where(core == 0, other, mine)

    drain()


def hand_over(*refs):
    half = len(refs) // 2
    for src, dst in zip(refs[:half], refs[half:]):
        dst[...] = src[...]


def per_device(
    enc_rows, pred_rows, enc_weight, pred_weight, out_weight, teacher, label_ids, frame_lengths, label_lengths
):
    vmem, smem, anywhere = (pl.BlockSpec(memory_space=s) for s in (pltpu.VMEM, pltpu.SMEM, pl.ANY))
    scratch = [
        pltpu.VMEM((UTTS, FRAMES, JOINT), BF16),
        pltpu.VMEM((LABELS, UTTS, JOINT), BF16),
        pltpu.VMEM((CHUNKS, VOCAB), BF16),
        pltpu.VMEM((CHUNKS, BLOCKS * 16, 128), BF16),
        pltpu.VMEM((JOINT, VOCAB), BF16),
        pltpu.VMEM((BLOCKS * 16, 128), F32),
        pltpu.VMEM((PADDED, JOINT), BF16),
        pltpu.VMEM((JOINT, PADDED), BF16),
        pltpu.VMEM((PADDED, JOINT), F32),
        pltpu.VMEM((PAIRS, VOCAB), F32),
        pltpu.VMEM((PAIRS, VOCAB), F32),
        pltpu.VMEM((PADDED, VOCAB), BF16),
        pltpu.VMEM((UTTS * LABELS, FRAMES, VOCAB), BF16),
        pltpu.VMEM((JOINT, JOINT), BF16),
        pltpu.VMEM((JOINT, JOINT), BF16),
        pltpu.VMEM((JOINT, JOINT), BF16),
        pltpu.VMEM((128, JOINT), F32),
        pltpu.VMEM((PAIRS, 128), F32),
        pltpu.VMEM((PAIRS, 128), F32),
        pltpu.VMEM((CHUNKS, BLOCKS * 16, 128), F32),
        pltpu.VMEM((CHUNKS, CODED, 128), jnp.int16),
        pltpu.VMEM((CHUNKS, CODED, 128), jnp.int16),
        pltpu.VMEM((CHUNKS, 3 * (128 + 16), 128), jnp.int16),
        pltpu.VMEM((CHUNKS, 3 * (128 + 16), 128), jnp.int16),
        pltpu.VMEM((7, 128, 128), jnp.int16),
        pltpu.VMEM((7, 128, 128), jnp.int16),
        pltpu.VMEM((2 * SIDE, JOINT), F32),
        pltpu.VMEM((2, 240, 128), jnp.int16),
        pltpu.VMEM((SIDE, JOINT), F32),
        pltpu.VMEM((3, 144, 128), jnp.int16),
        pltpu.VMEM((3, 96, 128), jnp.int16),
        pltpu.VMEM((1, 144, 128), jnp.int16),
        pltpu.VMEM((3, 96, 128), jnp.int16),
        pltpu.VMEM((SIDE, JOINT), F32),
        pltpu.VMEM((SIDE, JOINT), F32),
        pltpu.VMEM((SIDE, JOINT), F32),
        pltpu.VMEM((CHUNKS, 16, 128), F32),
        pltpu.SemaphoreType.DMA((6,)),
        pltpu.SemaphoreType.DMA((144,)),
        pltpu.SemaphoreType.DMA((144,)),
    ]
    shapes = (
        jax.ShapeDtypeStruct((LABELS, UTTS, FRAMES), F32),
        jax.ShapeDtypeStruct((UTTS, FRAMES, JOINT), F32),
        jax.ShapeDtypeStruct((LABELS, UTTS, JOINT), F32),
        jax.ShapeDtypeStruct((CHUNKS, VOCAB), F32),
    )
    results = pl.pallas_call(
        kernel,
        out_shape=shapes,
        in_specs=[smem] * 3 + [anywhere] * 6,
        out_specs=(vmem,) * 4,
        scratch_shapes=scratch,
        compiler_params=pltpu.CompilerParams(
            collective_id=0, has_side_effects=True, vmem_limit_bytes=56 * 1024 * 1024
        ),
    )(
        frame_lengths, label_lengths, label_ids, enc_rows, pred_rows.transpose(1, 0, 2), out_weight,
        enc_weight, pred_weight, teacher.transpose(0, 2, 1, 3).reshape(UTTS * LABELS, FRAMES, VOCAB),
    )
    loss, grad_enc, grad_pred, grad_out = pl.pallas_call(
        hand_over, out_shape=shapes, in_specs=[vmem] * 4, out_specs=(vmem,) * 4
    )(*results)
    return loss.transpose(1, 2, 0), grad_enc, grad_pred.transpose(1, 0, 2), grad_out


def solution(mesh):
    return jax.shard_map(
        per_device,
        mesh=mesh,
        in_specs=(
            P(None, "tm", None),
            P(None, "label", None),
            P(),
            P(),
            P(("tm", "label"), "vocab"),
            P(None, "tm", "label", "vocab"),
            P(None, "label"),
            P(),
            P(),
        ),
        out_specs=(
            P(None, "tm", "label"),
            P(None, "tm", None),
            P(None, "label", None),
            P(("tm", "label"), "vocab"),
        ),
        check_vma=False,
    )
```

```python
import functools

import jax
import jax.numpy as jnp
from jax import lax
from jax.experimental import pallas as pl
from jax.experimental.pallas import tpu as pltpu
from jax.sharding import PartitionSpec as P

MESH = pl.DeviceIdType.MESH
F32, BF16 = jnp.float32, jnp.bfloat16
label_weight = 0.5

SIZE = {"x": 4, "y": 4, "z": 8}
ORDERS = (("z", "y", "x"), ("z", "y", "x"), ("z", "x", "y"), ("z", "x", "y"), ("y", "x", "z"))
CHUNKS = len(ORDERS)
TRAVEL = (4, 0, 2, 1, 3)
SLOT = (0, 3, 1, 4, 2)
GATHER = (4, 0, 2, 1, 3)
PARTS = ((0, 2), (4,), (1, 3))
BLOCKS = 128
UTTS, FRAMES, LABELS = 2, 24, 10
ROWS = UTTS * FRAMES
PAIRS = ROWS * LABELS
PADDED = 512
JOINT = 640
VOCAB = 2048
TILES = VOCAB // 128
SIDE = 40
CODED = 7 * (256 + 16)
LEVELS = 32767.0


def distances(axis):
    n = SIZE[axis]
    return sorted(range(1, n), key=lambda d: -min(d, n - d))


def nt(a, b):
    return lax.dot_general(a, b, (((1,), (1,)), ((), ())), preferred_element_type=F32)


def nn(a, b):
    return jnp.dot(a, b, preferred_element_type=F32)


def split3(value):
    first = value.astype(BF16)
    rest = value - first.astype(F32)
    second = rest.astype(BF16)
    third = (rest - second.astype(F32)).astype(BF16)
    return first, second, third


def encode(block):
    rows = block.shape[0]
    tiles = block.reshape(rows // 16, 16, 128)
    peak = jnp.maximum(jnp.max(jnp.abs(tiles), axis=0), 1e-35)
    power = jnp.ceil(jnp.log2(peak) + 0.01)
    codes = jnp.round(tiles * (LEVELS * jnp.exp2(-power))[None]).reshape(rows, 128)
    return codes.astype(jnp.int32).astype(jnp.int16), power.astype(jnp.int32).astype(jnp.int16)


def decode(codes, power):
    rows = codes.shape[0]
    scale = jnp.exp2(power.astype(jnp.int32).astype(F32)) * (1.0 / LEVELS)
    tiles = codes.astype(jnp.int32).astype(F32).reshape(rows // 16, 16, 128)
    return (tiles * scale[None]).reshape(rows, 128)


def kernel(
    frame_len_hbm, label_len_hbm, ids_hbm, enc_rows_hbm, pred_rows_hbm, own_weight_hbm, enc_weight_hbm, pred_weight_hbm, teacher_hbm,
    loss_out, enc_out, pred_out, grad_out,
    frame_len, label_len, ids, enc_rows, pred_rows, own_weight, raw, weight, wide, hidden, hidden_t, act, post, expo, dlog, teacher, enc_weight, pred_weight, perm,
    proj, stats, stats_in, term, coded, coded_in, mid_coded, mid_in, last_code, last_in,
    side, side_code, pair_in, y_in, x_in, zh_in, zl_in, side_nat, grads, grads_in, result,
    local_sem, send_sem, recv_sem,
):
    tm, lab, core = lax.axis_index("tm"), lax.axis_index("label"), lax.axis_index("vocab")
    at = {"x": tm // 4, "y": lab // 2, "z": (lab % 2) * 4 + tm % 4}

    def device(axis, coordinate):
        where = dict(at)
        where[axis] = coordinate
        return (where["x"] * 4 + where["z"] % 4, where["y"] * 2 + where["z"] // 4, core)

    def around(axis, distance):
        return lax.rem(at[axis] + distance, SIZE[axis])

    other_core = (tm, lab, 1 - core)
    sent = []

    def send(src, dst, target):
        number = len(sent)
        copy = pltpu.make_async_remote_copy(
            src_ref=src, dst_ref=dst, send_sem=send_sem.at[number], recv_sem=recv_sem.at[number],
            device_id=target, device_id_type=MESH,
        )
        copy.start()
        sent.append(copy)
        return copy

    left = [0]

    def drain():
        for copy in sent[left[0] :]:
            copy.wait_send()
        left[0] = len(sent)

    def arrived(copies):
        for copy in copies:
            copy.wait_recv()

    barrier = pltpu.get_barrier_semaphore()
    partners = [device(a, around(a, d)) for a in "zyx" for d in distances(a)] + [other_core]
    for target in partners:
        pl.semaphore_signal(barrier, inc=1, device_id=target, device_id_type=MESH)

    local = []
    moves = (
        (own_weight_hbm, own_weight), (enc_rows_hbm, enc_rows), (pred_rows_hbm, pred_rows),
        (enc_weight_hbm, enc_weight), (pred_weight_hbm, pred_weight), (teacher_hbm, teacher),
        (frame_len_hbm, frame_len), (label_len_hbm, label_len), (ids_hbm, ids),
    )
    for number, (src, dst) in enumerate(moves):
        copy = pltpu.make_async_copy(src, dst, local_sem.at[number])
        copy.start()
        local.append(copy)

    local[0].wait()
    own = own_weight[...].astype(F32)
    for r in range(CHUNKS):
        for c in range(TILES):
            result[r, c : c + 1, :] = own[r : r + 1, c * 128 : (c + 1) * 128]

    def spot(r):
        first, middle, last = ORDERS[r]
        return (at[last] * SIZE[middle] + at[middle]) * SIZE[first] + at[first]

    for r in range(CHUNKS):
        raw[r, pl.ds(pl.multiple_of(spot(r) * 16, 16), 16), :] = result[r].astype(BF16)

    pl.semaphore_wait(barrier, len(partners))

    first_copies = {}
    for low, high in ((0, 2), (2, 4), (4, 5)):
        axis = ORDERS[low][0]
        block = raw.at[low:high, pl.ds(pl.multiple_of(spot(low) * 16, 16), 16), :]
        first_copies[low] = [send(block, block, device(axis, around(axis, d))) for d in distances(axis)]

    j = lax.broadcasted_iota(jnp.int32, (JOINT, BLOCKS), 0)
    block_at = lax.broadcasted_iota(jnp.int32, (JOINT, BLOCKS), 1)
    for r in range(CHUNKS):
        first, middle, last = ORDERS[r]
        n1, n2 = SIZE[first], SIZE[middle]
        coords = {first: block_at % n1, middle: (block_at // n1) % n2, last: block_at // (n1 * n2)}
        natural = coords["x"] * 32 + (coords["z"] % 4) * 8 + coords["y"] * 2 + coords["z"] // 4
        columns = slice(SLOT[r] * BLOCKS, (SLOT[r] + 1) * BLOCKS)
        perm[:, columns] = jnp.where(j == natural * CHUNKS + r, 1.0, 0.0).astype(BF16)

    second_copies = {}
    for r in GATHER:
        first, middle, last = ORDERS[r]
        if r in first_copies:
            arrived(first_copies[r])
        rows = SIZE[first] * 16
        block = raw.at[r, pl.ds(pl.multiple_of((at[last] * SIZE[middle] + at[middle]) * rows, 16), rows), :]
        second_copies[r] = [send(block, block, device(middle, around(middle, d))) for d in distances(middle)]

    for copy in local[1:5]:
        copy.wait()
    proj[...] = jnp.zeros_like(proj)
    for b in range(UTTS):
        proj[b * FRAMES : (b + 1) * FRAMES, :] = enc_rows[b].astype(F32)
    for u in range(LABELS):
        proj[ROWS + UTTS * u : ROWS + UTTS * (u + 1), :] = pred_rows[u].astype(F32)
    proj[0:ROWS, :] = nn(proj[0:ROWS, :].astype(BF16), enc_weight[...])
    proj[ROWS : ROWS + 32, :] = nn(proj[ROWS : ROWS + 32, :].astype(BF16), pred_weight[...])
    proj[...] = sum(nn(part, perm[...]) for part in split3(proj[...]))

    def last_block(r, coordinate):
        first, middle, last = ORDERS[r]
        rows = SIZE[first] * SIZE[middle] * 16
        return pl.ds(pl.multiple_of(coordinate * rows, 16), rows)

    def part_block(r, coordinate, half):
        first, middle, last = ORDERS[r]
        rows = SIZE[first] * SIZE[middle] * 16
        return pl.ds(pl.multiple_of(coordinate * rows + half * (rows // 2), 16), rows // 2)

    third_copies = {}
    for r in GATHER:
        last = ORDERS[r][2]
        arrived(second_copies[r])
        block = raw.at[r, last_block(r, at[last]), :]
        third_copies[r] = {
            d: send(block, block, device(last, around(last, SIZE[last] + d))) for d in ((2, -2, 1, -1) if SIZE[last] == 8 else (1, -1))
        }

    def hand_on(r):
        last = ORDERS[r][2]
        n = SIZE[last]
        near = n // 4
        copies = third_copies[r]
        more = []
        for way, half in ((1, 0), (-1, 1)):
            copies[way * near].wait_recv()
            source = around(last, n - way * near)
            place = part_block(r, source, half)
            block = raw.at[r, place, :]
            more.append(send(block, block, device(last, around(last, n + way * near))))
            if n == 8:
                block = raw.at[r, last_block(r, source), :]
                more.append(send(block, block, device(last, around(last, n + way))))
        third_copies[r] = more + ([copies[1], copies[-1]] if n == 8 else [])

    for b in range(UTTS):
        for u in range(LABELS):
            start = (b * LABELS + u) * FRAMES
            row = ROWS + UTTS * u + b
            act[start : start + FRAMES, :] = jnp.tanh(proj[b * FRAMES : (b + 1) * FRAMES, :] + proj[row : row + 1, :])
    act[PAIRS:PADDED, :] = jnp.zeros((PADDED - PAIRS, JOINT), F32)
    hidden[...] = act[...].astype(BF16)
    hidden_t[...] = act[...].T.astype(BF16)

    for copy in local[5:]:
        copy.wait()
    lanes = lax.broadcasted_iota(jnp.int32, (FRAMES, 128), 1)
    rows_at = lax.broadcasted_iota(jnp.int32, (FRAMES, 128), 0)

    def group(g):
        return pl.ds(pl.multiple_of(g * FRAMES, 8), FRAMES)

    def teacher_step(g, carry):
        total, ent = jnp.zeros((FRAMES, 128), F32), jnp.zeros((FRAMES, 128), F32)
        for c in range(TILES):
            part = teacher[g, :, c * 128 : (c + 1) * 128].astype(F32)
            post[group(g), c * 128 : (c + 1) * 128] = part
            total += part
            ent += part * jnp.log(part)
        total = jnp.sum(total, axis=1, keepdims=True)
        ent = jnp.sum(ent, axis=1, keepdims=True)
        stats[group(g), :] = jnp.where(lanes == 1, total, jnp.where(lanes == 2, ent, 0.0))
        return carry

    lax.fori_loop(0, 10, teacher_step, 0)
    for r in GATHER[:3]:
        hand_on(r)
    lax.fori_loop(10, UTTS * LABELS, teacher_step, 0)
    dlog[PAIRS:PADDED, :] = jnp.zeros((PADDED - PAIRS, VOCAB), BF16)
    for r in GATHER[3:]:
        hand_on(r)

    def settle(r):
        arrived(third_copies[r])
        wide[...] = raw[r].astype(F32)
        base = SLOT[r] * BLOCKS
        for c in range(TILES):
            weight[base : base + BLOCKS, c * 128 : (c + 1) * 128] = wide[pl.ds(c, BLOCKS, stride=16), :].astype(BF16)

    done = 0
    for rows in PARTS:
        for r in rows:
            settle(r)
        depth = slice(done, done + len(rows) * BLOCKS)
        done += len(rows) * BLOCKS
        for start in range(0, VOCAB, 512):
            columns = slice(start, start + 512)
            product = nn(hidden[0:PAIRS, depth], weight[depth, columns])
            expo[:, columns] = product if depth.start == 0 else expo[:, columns] + product

    def local_id(g):
        utt = g // LABELS
        return ids[utt, g - LABELS * utt] - core * VOCAB

    def expo_step(g, carry):
        rows = group(g)
        emitted = local_id(g)
        zero = jnp.zeros((FRAMES, 128), F32)
        expsum, cross, picked = zero, zero, zero
        for c in range(TILES):
            columns = slice(c * 128, (c + 1) * 128)
            logits = expo[rows, columns]
            powers = jnp.exp(logits)
            expo[rows, columns] = powers
            expsum += powers
            cross += post[rows, columns] * logits
            picked += jnp.where(lanes == emitted - c * 128, logits, 0.0)
        expsum = jnp.sum(expsum, axis=1, keepdims=True)
        cross = jnp.sum(cross, axis=1, keepdims=True)
        picked = jnp.sum(picked, axis=1, keepdims=True)
        stats[rows, :] += jnp.where(lanes == 0, expsum, jnp.where(lanes == 3, cross, jnp.where(lanes == 4, picked, 0.0)))
        return carry

    lax.fori_loop(0, UTTS * LABELS, expo_step, 0, unroll=10)
    stats_copy = send(stats, stats_in, other_core)
    stats_copy.wait_recv()

    def valid(g):
        utt = g // LABELS
        frames, labels = jnp.where(utt == 1, frame_len[1], frame_len[0]), jnp.where(utt == 1, label_len[1], label_len[0])
        label_ok = jnp.where(lab * LABELS + g - LABELS * utt < labels, 1.0, 0.0)
        return jnp.where(tm * FRAMES + rows_at < frames, label_ok, 0.0)

    def dlog_step(pair, carry):
        scales = []
        for half in range(2):
            g = 2 * pair + half
            sums = stats[group(g), :] + stats_in[group(g), :]
            mask = valid(g)
            scales.append(
                (
                    (1.0 + label_weight) * mask / sums[:, 0:1],
                    mask / sums[:, 1:2],
                    label_weight * mask,
                    local_id(g),
                    group(g),
                )
            )
        for c in range(TILES):
            columns = slice(c * 128, (c + 1) * 128)
            parts = []
            for a, b, hot, emitted, rows in scales:
                value = a * expo[rows, columns] - b * post[rows, columns]
                parts.append(value - jnp.where(lanes == emitted - c * 128, hot, 0.0))
            dlog[pl.ds(pl.multiple_of(pair * 2 * FRAMES, 16), 2 * FRAMES), columns] = jnp.concatenate(parts, axis=0).astype(BF16)
        return carry

    lax.fori_loop(0, UTTS * LABELS // 2, dlog_step, 0, unroll=5)

    def ship(r, source, store, inbox, axis, rows, base):
        copies = []
        for d in distances(axis):
            start = base + around(axis, d) * rows
            codes, power = encode(source[r, pl.ds(pl.multiple_of(start, 16), rows), :])
            low = (d - 1) * (rows + 16)
            store[r, low : low + rows, :] = codes
            store[r, low + rows : low + rows + 16, :] = power
            place = slice(low, low + rows + 16)
            copies.append(send(store.at[r, place, :], inbox.at[r, place, :], device(axis, around(axis, d))))
        return copies

    def collect(r, copies, inbox, axis, rows, base):
        arrived(copies)
        place = pl.ds(pl.multiple_of(base + at[axis] * rows, 16), rows)
        total = term[r, place, :]
        for d in range(1, SIZE[axis]):
            low = (d - 1) * (rows + 16)
            total = total + decode(inbox[r, low : low + rows, :], inbox[r, low + rows : low + rows + 16, :])
        term[r, place, :] = total

    def sizes(r):
        first, middle, last = ORDERS[r]
        low = SIZE[first] * 16
        high = low * SIZE[middle]
        return low, high, at[last] * high, at[last] * high + at[middle] * low

    gathered = len(sent)
    third = {}

    def multiply(r):
        base = SLOT[r] * BLOCKS
        product = nn(hidden_t[base : base + BLOCKS, :], dlog[...])
        for c in range(TILES):
            term[r, pl.ds(c, BLOCKS, stride=16), :] = product[:, c * 128 : (c + 1) * 128]

    def depart(r):
        third[r] = ship(r, term, coded, coded_in, ORDERS[r][2], sizes(r)[1], 0)

    for r in (4, 0, 2):
        multiply(r)
        depart(r)

    act[...] = nt(dlog[...], weight[...]) * (1.0 - act[...] * act[...])
    side[...] = jnp.zeros_like(side)
    for b in range(UTTS):
        over_labels = jnp.zeros((FRAMES, JOINT), F32)
        for u in range(LABELS):
            start = (b * LABELS + u) * FRAMES
            part = act[start : start + FRAMES, :]
            over_labels += part
            row = b * SIDE + FRAMES + u
            side[row : row + 1, :] = jnp.sum(part, axis=0, keepdims=True)
        side[b * SIDE : b * SIDE + FRAMES, :] = over_labels
    theirs = side.at[pl.ds(pl.multiple_of((1 - core) * SIDE, 8), SIDE), :]
    pair_copy = send(theirs, pair_in, other_core)

    second, first_hop = {}, {}

    def turn(r):
        low, high, start, _ = sizes(r)
        collect(r, third[r], coded_in, ORDERS[r][2], high, 0)
        second[r] = ship(r, term, mid_coded, mid_in, ORDERS[r][1], low, start)

    def finish(low, high):
        axis = ORDERS[low][0]
        size, _, start, place = sizes(low)
        for r in range(low, high):
            collect(r, second[r], mid_in, ORDERS[r][1], size, start)
        first_hop[low] = []
        rows, base = (high - low) * 16, low * 24
        for d in distances(axis):
            spot_d = pl.ds(pl.multiple_of(place + around(axis, d) * 16, 16), 16)
            codes, power = encode(jnp.concatenate([term[r, spot_d, :] for r in range(low, high)], axis=0))
            last_code[d - 1, base : base + rows, :] = codes
            last_code[d - 1, base + rows : base + rows + 16, :] = power
            block = slice(base, base + rows + 16)
            first_hop[low].append(send(last_code.at[d - 1, block, :], last_in.at[d - 1, block, :], device(axis, around(axis, d))))

    for copy in sent[:gathered]:
        copy.wait_send()
    left[0] = gathered

    multiply(1)
    pair_copy.wait_recv()
    side_nat[...] = side[pl.ds(pl.multiple_of(core * SIDE, 8), SIDE), :] + pair_in[...]

    def fold(start, rows):
        strips = [side_nat[start : start + rows, k * 128 : (k + 1) * 128] for k in range(JOINT // 128)]
        if rows == FRAMES:
            strips.append(jnp.zeros((8, 128), F32))
        return jnp.concatenate(strips, axis=0)

    def code_side(slot):
        for start, rows, span, low in ((0, FRAMES, 128, 0), (FRAMES, SIDE - FRAMES, 80, 144)):
            codes, power = encode(fold(start, rows))
            side_code[slot, low : low + span, :] = codes
            side_code[slot, low + span : low + span + 16, :] = power

    def add_side(enc_ref, enc_count, pred_ref, pred_count):
        for ref, count, start, rows, span in ((enc_ref, enc_count, 0, FRAMES, 128), (pred_ref, pred_count, FRAMES, SIDE - FRAMES, 80)):
            total = decode(ref[0, 0:span, :], ref[0, span : span + 16, :])
            for d in range(1, count):
                total = total + decode(ref[d, 0:span, :], ref[d, span : span + 16, :])
            for k in range(JOINT // 128):
                side_nat[start : start + rows, k * 128 : (k + 1) * 128] += total[k * rows : (k + 1) * rows]

    code_side(0)
    enc_part, pred_part = side_code.at[0, 0:144, :], side_code.at[0, 144:240, :]
    y_copies = [send(enc_part, y_in.at[d - 1], device("y", around("y", d))) for d in distances("y")]
    x_copies = [send(pred_part, x_in.at[d - 1], device("x", around("x", d))) for d in distances("x")]

    depart(1)
    multiply(3)
    depart(3)

    for b in range(UTTS):
        for u in range(LABELS):
            g = b * LABELS + u
            rows = slice(g * FRAMES, (g + 1) * FRAMES)
            sums = stats[rows, :] + stats_in[rows, :]
            expsum, total, ent, cross, picked = (sums[:, k : k + 1] for k in range(5))
            lse = jnp.log(expsum)
            pair_loss = ent / total - jnp.log(total) - cross / total + lse + label_weight * (lse - picked)
            line = jnp.sum(jnp.where(lanes == rows_at, valid(g) * pair_loss, 0.0), axis=0, keepdims=True)
            loss_out[u, b : b + 1, :] = line[:, 0:FRAMES]

    turn(0)
    turn(2)

    arrived(y_copies + x_copies)
    add_side(y_in, 3, x_in, 3)
    code_side(1)
    z_low, z_high = at["z"] % 4, at["z"] // 4
    zh_copy = send(side_code.at[1, 0:144, :], zh_in.at[0], device("z", around("z", 4)))
    zl_copies = [
        send(side_code.at[1, 144:240, :], zl_in.at[d - 1], device("z", z_high * 4 + (z_low + d) % 4)) for d in range(1, 4)
    ]

    turn(4)
    turn(1)
    turn(3)
    finish(4, 5)

    finish(0, 2)
    finish(2, 4)

    def stacked(value):
        return jnp.concatenate([part.astype(F32) for part in split3(value)], axis=0).astype(BF16)

    def unstacked(value):
        rows = value.shape[0] // 3
        return value[0:rows] + value[rows : 2 * rows] + value[2 * rows : 3 * rows]

    arrived([zh_copy] + zl_copies)
    add_side(zh_in, 1, zl_in, 3)
    natural = unstacked(nt(stacked(side_nat[...]), perm[...]))
    grads[0:FRAMES, :] = unstacked(nt(stacked(natural[0:FRAMES]), enc_weight[...]))
    grads[FRAMES:SIDE, :] = unstacked(nt(stacked(natural[FRAMES:SIDE]), pred_weight[...]))
    grads_copy = send(grads, grads_in, other_core)

    for low, high in ((4, 5), (0, 2), (2, 4)):
        arrived(first_hop[low])
        rows, base = (high - low) * 16, low * 24
        total = jnp.concatenate(
            [term[r, pl.ds(pl.multiple_of(spot(r) * 16, 16), 16), :] for r in range(low, high)], axis=0
        )
        for d in distances(ORDERS[low][0]):
            total = total + decode(last_in[d - 1, base : base + rows, :], last_in[d - 1, base + rows : base + rows + 16, :])
        for r in range(low, high):
            result[r] = total[(r - low) * 16 : (r - low + 1) * 16]
            for c in range(TILES):
                grad_out[r : r + 1, c * 128 : (c + 1) * 128] = result[r, c : c + 1, :]

    grads_copy.wait_recv()
    enc_out[core] = grads[0:FRAMES, :]
    enc_out[1 - core] = grads_in[0:FRAMES, :]
    for u in range(LABELS):
        mine, other = grads[FRAMES + u : FRAMES + u + 1, :], grads_in[FRAMES + u : FRAMES + u + 1, :]
        pred_out[u, 0:1, :] = jnp.where(core == 0, mine, other)
        pred_out[u, 1:2, :] = jnp.where(core == 0, other, mine)

    drain()


def hand_over(*refs):
    half = len(refs) // 2
    for src, dst in zip(refs[:half], refs[half:]):
        dst[...] = src[...]


def per_device(
    enc_rows, pred_rows, enc_weight, pred_weight, out_weight, teacher, label_ids, frame_lengths, label_lengths
):
    vmem, anywhere = (pl.BlockSpec(memory_space=s) for s in (pltpu.VMEM, pl.ANY))
    scratch = [
        pltpu.SMEM((UTTS,), jnp.int32),
        pltpu.SMEM((UTTS,), jnp.int32),
        pltpu.SMEM((UTTS, LABELS), jnp.int32),
        pltpu.VMEM((UTTS, FRAMES, JOINT), BF16),
        pltpu.VMEM((LABELS, UTTS, JOINT), BF16),
        pltpu.VMEM((CHUNKS, VOCAB), BF16),
        pltpu.VMEM((CHUNKS, BLOCKS * 16, 128), BF16),
        pltpu.VMEM((JOINT, VOCAB), BF16),
        pltpu.VMEM((BLOCKS * 16, 128), F32),
        pltpu.VMEM((PADDED, JOINT), BF16),
        pltpu.VMEM((JOINT, PADDED), BF16),
        pltpu.VMEM((PADDED, JOINT), F32),
        pltpu.VMEM((PAIRS, VOCAB), F32),
        pltpu.VMEM((PAIRS, VOCAB), F32),
        pltpu.VMEM((PADDED, VOCAB), BF16),
        pltpu.VMEM((UTTS * LABELS, FRAMES, VOCAB), BF16),
        pltpu.VMEM((JOINT, JOINT), BF16),
        pltpu.VMEM((JOINT, JOINT), BF16),
        pltpu.VMEM((JOINT, JOINT), BF16),
        pltpu.VMEM((128, JOINT), F32),
        pltpu.VMEM((PAIRS, 128), F32),
        pltpu.VMEM((PAIRS, 128), F32),
        pltpu.VMEM((CHUNKS, BLOCKS * 16, 128), F32),
        pltpu.VMEM((CHUNKS, CODED, 128), jnp.int16),
        pltpu.VMEM((CHUNKS, CODED, 128), jnp.int16),
        pltpu.VMEM((CHUNKS, 3 * (128 + 16), 128), jnp.int16),
        pltpu.VMEM((CHUNKS, 3 * (128 + 16), 128), jnp.int16),
        pltpu.VMEM((7, 128, 128), jnp.int16),
        pltpu.VMEM((7, 128, 128), jnp.int16),
        pltpu.VMEM((2 * SIDE, JOINT), F32),
        pltpu.VMEM((2, 240, 128), jnp.int16),
        pltpu.VMEM((SIDE, JOINT), F32),
        pltpu.VMEM((3, 144, 128), jnp.int16),
        pltpu.VMEM((3, 96, 128), jnp.int16),
        pltpu.VMEM((1, 144, 128), jnp.int16),
        pltpu.VMEM((3, 96, 128), jnp.int16),
        pltpu.VMEM((SIDE, JOINT), F32),
        pltpu.VMEM((SIDE, JOINT), F32),
        pltpu.VMEM((SIDE, JOINT), F32),
        pltpu.VMEM((CHUNKS, 16, 128), F32),
        pltpu.SemaphoreType.DMA((9,)),
        pltpu.SemaphoreType.DMA((144,)),
        pltpu.SemaphoreType.DMA((144,)),
    ]
    shapes = (
        jax.ShapeDtypeStruct((LABELS, UTTS, FRAMES), F32),
        jax.ShapeDtypeStruct((UTTS, FRAMES, JOINT), F32),
        jax.ShapeDtypeStruct((LABELS, UTTS, JOINT), F32),
        jax.ShapeDtypeStruct((CHUNKS, VOCAB), F32),
    )
    results = pl.pallas_call(
        kernel,
        out_shape=shapes,
        in_specs=[anywhere] * 9,
        out_specs=(vmem,) * 4,
        scratch_shapes=scratch,
        compiler_params=pltpu.CompilerParams(
            collective_id=0, has_side_effects=True, vmem_limit_bytes=56 * 1024 * 1024
        ),
    )(
        frame_lengths, label_lengths, label_ids, enc_rows, pred_rows.transpose(1, 0, 2), out_weight,
        enc_weight, pred_weight, teacher.transpose(0, 2, 1, 3).reshape(UTTS * LABELS, FRAMES, VOCAB),
    )
    loss, grad_enc, grad_pred, grad_out = pl.pallas_call(
        hand_over, out_shape=shapes, in_specs=[vmem] * 4, out_specs=(vmem,) * 4
    )(*results)
    return loss.transpose(1, 2, 0), grad_enc, grad_pred.transpose(1, 0, 2), grad_out


def solution(mesh):
    return jax.shard_map(
        per_device,
        mesh=mesh,
        in_specs=(
            P(None, "tm", None),
            P(None, "label", None),
            P(),
            P(),
            P(("tm", "label"), "vocab"),
            P(None, "tm", "label", "vocab"),
            P(None, "label"),
            P(),
            P(),
        ),
        out_specs=(
            P(None, "tm", "label"),
            P(None, "tm", None),
            P(None, "label", None),
            P(("tm", "label"), "vocab"),
        ),
        check_vma=False,
    )
```

```python
import functools

import jax
import jax.numpy as jnp
from jax import lax
from jax.experimental import pallas as pl
from jax.experimental.pallas import tpu as pltpu
from jax.sharding import PartitionSpec as P

MESH = pl.DeviceIdType.MESH
F32, BF16 = jnp.float32, jnp.bfloat16
label_weight = 0.5

SIZE = {"x": 4, "y": 4, "z": 8}
ORDERS = (("z", "y", "x"), ("z", "y", "x"), ("z", "x", "y"), ("z", "x", "y"), ("y", "x", "z"))
CHUNKS = len(ORDERS)
TRAVEL = (4, 0, 2, 1, 3)
SLOT = (0, 3, 1, 4, 2)
GATHER = (4, 0, 2, 1, 3)
PARTS = ((0, 2), (4,), (1, 3))
BLOCKS = 128
UTTS, FRAMES, LABELS = 2, 24, 10
ROWS = UTTS * FRAMES
PAIRS = ROWS * LABELS
PADDED = 512
JOINT = 640
VOCAB = 2048
TILES = VOCAB // 128
SIDE = 40
CODED = 7 * (256 + 16)
LEVELS = 32767.0


def distances(axis):
    n = SIZE[axis]
    return sorted(range(1, n), key=lambda d: -min(d, n - d))


def nt(a, b):
    return lax.dot_general(a, b, (((1,), (1,)), ((), ())), preferred_element_type=F32)


def nn(a, b):
    return jnp.dot(a, b, preferred_element_type=F32)


def split3(value):
    first = value.astype(BF16)
    rest = value - first.astype(F32)
    second = rest.astype(BF16)
    third = (rest - second.astype(F32)).astype(BF16)
    return first, second, third


def encode(block):
    rows = block.shape[0]
    tiles = block.reshape(rows // 16, 16, 128)
    peak = jnp.maximum(jnp.max(jnp.abs(tiles), axis=0), 1e-35)
    power = jnp.ceil(jnp.log2(peak) + 0.01)
    codes = jnp.round(tiles * (LEVELS * jnp.exp2(-power))[None]).reshape(rows, 128)
    return codes.astype(jnp.int32).astype(jnp.int16), power.astype(jnp.int32).astype(jnp.int16)


def decode(codes, power):
    rows = codes.shape[0]
    scale = jnp.exp2(power.astype(jnp.int32).astype(F32)) * (1.0 / LEVELS)
    tiles = codes.astype(jnp.int32).astype(F32).reshape(rows // 16, 16, 128)
    return (tiles * scale[None]).reshape(rows, 128)


def kernel(
    frame_len_hbm, label_len_hbm, ids_hbm, enc_rows_hbm, pred_rows_hbm, own_weight_hbm, enc_weight_hbm, pred_weight_hbm, teacher_hbm,
    loss_out, enc_out, pred_out, grad_out,
    frame_len, label_len, ids, enc_rows, pred_rows, own_weight, raw, weight, wide, hidden, hidden_t, act, post, expo, dlog, teacher, enc_weight, pred_weight, perm,
    proj, stats, stats_in, term, coded, coded_in, mid_coded, mid_in, last_code, last_in,
    side, side_code, pair_in, y_in, x_in, zh_in, zl_in, side_nat, grads, grads_in, result,
    local_sem, send_sem, recv_sem,
):
    tm, lab, core = lax.axis_index("tm"), lax.axis_index("label"), lax.axis_index("vocab")
    at = {"x": tm // 4, "y": lab // 2, "z": (lab % 2) * 4 + tm % 4}

    def device(axis, coordinate):
        where = dict(at)
        where[axis] = coordinate
        return (where["x"] * 4 + where["z"] % 4, where["y"] * 2 + where["z"] // 4, core)

    def around(axis, distance):
        return lax.rem(at[axis] + distance, SIZE[axis])

    other_core = (tm, lab, 1 - core)
    sent = []

    def send(src, dst, target):
        number = len(sent)
        copy = pltpu.make_async_remote_copy(
            src_ref=src, dst_ref=dst, send_sem=send_sem.at[number], recv_sem=recv_sem.at[number],
            device_id=target, device_id_type=MESH,
        )
        copy.start()
        sent.append(copy)
        return copy

    left = [0]

    def drain():
        for copy in sent[left[0] :]:
            copy.wait_send()
        left[0] = len(sent)

    def arrived(copies):
        for copy in copies:
            copy.wait_recv()

    barrier = pltpu.get_barrier_semaphore()
    partners = [device(a, around(a, d)) for a in "zyx" for d in distances(a)] + [other_core]
    for target in partners:
        pl.semaphore_signal(barrier, inc=1, device_id=target, device_id_type=MESH)

    local = []
    moves = (
        (own_weight_hbm, own_weight), (enc_rows_hbm, enc_rows), (pred_rows_hbm, pred_rows),
        (enc_weight_hbm, enc_weight), (pred_weight_hbm, pred_weight), (teacher_hbm, teacher),
        (frame_len_hbm, frame_len), (label_len_hbm, label_len), (ids_hbm, ids),
    )
    for number, (src, dst) in enumerate(moves):
        copy = pltpu.make_async_copy(src, dst, local_sem.at[number])
        copy.start()
        local.append(copy)

    local[0].wait()
    own = own_weight[...].astype(F32)
    for r in range(CHUNKS):
        for c in range(TILES):
            result[r, c : c + 1, :] = own[r : r + 1, c * 128 : (c + 1) * 128]

    def spot(r):
        first, middle, last = ORDERS[r]
        return (at[last] * SIZE[middle] + at[middle]) * SIZE[first] + at[first]

    for r in range(CHUNKS):
        raw[r, pl.ds(pl.multiple_of(spot(r) * 16, 16), 16), :] = result[r].astype(BF16)

    pl.semaphore_wait(barrier, len(partners))

    first_copies = {}
    for low, high in ((0, 2), (2, 4), (4, 5)):
        axis = ORDERS[low][0]
        block = raw.at[low:high, pl.ds(pl.multiple_of(spot(low) * 16, 16), 16), :]
        first_copies[low] = [send(block, block, device(axis, around(axis, d))) for d in distances(axis)]

    j = lax.broadcasted_iota(jnp.int32, (JOINT, BLOCKS), 0)
    block_at = lax.broadcasted_iota(jnp.int32, (JOINT, BLOCKS), 1)
    for r in range(CHUNKS):
        first, middle, last = ORDERS[r]
        n1, n2 = SIZE[first], SIZE[middle]
        coords = {first: block_at % n1, middle: (block_at // n1) % n2, last: block_at // (n1 * n2)}
        natural = coords["x"] * 32 + (coords["z"] % 4) * 8 + coords["y"] * 2 + coords["z"] // 4
        columns = slice(SLOT[r] * BLOCKS, (SLOT[r] + 1) * BLOCKS)
        perm[:, columns] = jnp.where(j == natural * CHUNKS + r, 1.0, 0.0).astype(BF16)

    second_copies = {}
    for r in GATHER:
        first, middle, last = ORDERS[r]
        if r in first_copies:
            arrived(first_copies[r])
        rows = SIZE[first] * 16
        block = raw.at[r, pl.ds(pl.multiple_of((at[last] * SIZE[middle] + at[middle]) * rows, 16), rows), :]
        second_copies[r] = [send(block, block, device(middle, around(middle, d))) for d in distances(middle)]

    for copy in local[1:5]:
        copy.wait()
    proj[...] = jnp.zeros_like(proj)
    for b in range(UTTS):
        proj[b * FRAMES : (b + 1) * FRAMES, :] = enc_rows[b].astype(F32)
    for u in range(LABELS):
        proj[ROWS + UTTS * u : ROWS + UTTS * (u + 1), :] = pred_rows[u].astype(F32)
    proj[0:ROWS, :] = nn(proj[0:ROWS, :].astype(BF16), enc_weight[...])
    proj[ROWS : ROWS + 32, :] = nn(proj[ROWS : ROWS + 32, :].astype(BF16), pred_weight[...])
    proj[...] = sum(nn(part, perm[...]) for part in split3(proj[...]))

    def last_block(r, coordinate):
        first, middle, last = ORDERS[r]
        rows = SIZE[first] * SIZE[middle] * 16
        return pl.ds(pl.multiple_of(coordinate * rows, 16), rows)

    def part_block(r, coordinate, half):
        first, middle, last = ORDERS[r]
        rows = SIZE[first] * SIZE[middle] * 16
        return pl.ds(pl.multiple_of(coordinate * rows + half * (rows // 2), 16), rows // 2)

    third_copies = {}
    for r in GATHER:
        last = ORDERS[r][2]
        arrived(second_copies[r])
        block = raw.at[r, last_block(r, at[last]), :]
        third_copies[r] = {
            d: send(block, block, device(last, around(last, SIZE[last] + d))) for d in ((2, -2, 1, -1) if SIZE[last] == 8 else (1, -1))
        }

    def hand_on(r):
        last = ORDERS[r][2]
        n = SIZE[last]
        near = n // 4
        copies = third_copies[r]
        more = []
        for way, half in ((1, 0), (-1, 1)):
            copies[way * near].wait_recv()
            source = around(last, n - way * near)
            place = part_block(r, source, half)
            block = raw.at[r, place, :]
            more.append(send(block, block, device(last, around(last, n + way * near))))
            if n == 8:
                block = raw.at[r, last_block(r, source), :]
                more.append(send(block, block, device(last, around(last, n + way))))
        third_copies[r] = more + ([copies[1], copies[-1]] if n == 8 else [])

    for b in range(UTTS):
        for u in range(LABELS):
            start = (b * LABELS + u) * FRAMES
            row = ROWS + UTTS * u + b
            act[start : start + FRAMES, :] = jnp.tanh(proj[b * FRAMES : (b + 1) * FRAMES, :] + proj[row : row + 1, :])
    act[PAIRS:PADDED, :] = jnp.zeros((PADDED - PAIRS, JOINT), F32)
    hidden[...] = act[...].astype(BF16)
    hidden_t[...] = act[...].T.astype(BF16)

    for copy in local[5:]:
        copy.wait()
    lanes = lax.broadcasted_iota(jnp.int32, (FRAMES, 128), 1)
    rows_at = lax.broadcasted_iota(jnp.int32, (FRAMES, 128), 0)

    def group(g):
        return pl.ds(pl.multiple_of(g * FRAMES, 8), FRAMES)

    def teacher_step(g, carry):
        total, ent = jnp.zeros((FRAMES, 128), F32), jnp.zeros((FRAMES, 128), F32)
        for c in range(TILES):
            part = teacher[g, :, c * 128 : (c + 1) * 128].astype(F32)
            post[group(g), c * 128 : (c + 1) * 128] = part
            total += part
            ent += part * jnp.log(part)
        total = jnp.sum(total, axis=1, keepdims=True)
        ent = jnp.sum(ent, axis=1, keepdims=True)
        stats[group(g), :] = jnp.where(lanes == 1, total, jnp.where(lanes == 2, ent, 0.0))
        return carry

    lax.fori_loop(0, 10, teacher_step, 0)
    for r in GATHER[:3]:
        hand_on(r)
    lax.fori_loop(10, UTTS * LABELS, teacher_step, 0)
    dlog[PAIRS:PADDED, :] = jnp.zeros((PADDED - PAIRS, VOCAB), BF16)
    for r in GATHER[3:]:
        hand_on(r)

    def settle(r):
        arrived(third_copies[r])
        wide[...] = raw[r].astype(F32)
        base = SLOT[r] * BLOCKS
        for c in range(TILES):
            weight[base : base + BLOCKS, c * 128 : (c + 1) * 128] = wide[pl.ds(c, BLOCKS, stride=16), :].astype(BF16)

    done = 0
    for rows in PARTS:
        for r in rows:
            settle(r)
        depth = slice(done, done + len(rows) * BLOCKS)
        done += len(rows) * BLOCKS
        for start in range(0, VOCAB, 512):
            columns = slice(start, start + 512)
            product = nn(hidden[0:PAIRS, depth], weight[depth, columns])
            expo[:, columns] = product if depth.start == 0 else expo[:, columns] + product

    def local_id(g):
        utt = g // LABELS
        return ids[utt, g - LABELS * utt] - core * VOCAB

    def expo_step(g, carry):
        rows = group(g)
        emitted = local_id(g)
        zero = jnp.zeros((FRAMES, 128), F32)
        expsum, cross, picked = zero, zero, zero
        for c in range(TILES):
            columns = slice(c * 128, (c + 1) * 128)
            logits = expo[rows, columns]
            powers = jnp.exp(logits)
            expo[rows, columns] = powers
            expsum += powers
            cross += post[rows, columns] * logits
            picked += jnp.where(lanes == emitted - c * 128, logits, 0.0)
        expsum = jnp.sum(expsum, axis=1, keepdims=True)
        cross = jnp.sum(cross, axis=1, keepdims=True)
        picked = jnp.sum(picked, axis=1, keepdims=True)
        stats[rows, :] += jnp.where(lanes == 0, expsum, jnp.where(lanes == 3, cross, jnp.where(lanes == 4, picked, 0.0)))
        return carry

    stats_copies = []
    for b in range(UTTS):
        lax.fori_loop(b * LABELS, (b + 1) * LABELS, expo_step, 0, unroll=10)
        rows = slice(b * LABELS * FRAMES, (b + 1) * LABELS * FRAMES)
        stats_copies.append(send(stats.at[rows, :], stats_in.at[rows, :], other_core))

    def valid(g):
        utt = g // LABELS
        frames, labels = jnp.where(utt == 1, frame_len[1], frame_len[0]), jnp.where(utt == 1, label_len[1], label_len[0])
        label_ok = jnp.where(lab * LABELS + g - LABELS * utt < labels, 1.0, 0.0)
        return jnp.where(tm * FRAMES + rows_at < frames, label_ok, 0.0)

    def dlog_step(pair, carry):
        scales = []
        for half in range(2):
            g = 2 * pair + half
            sums = stats[group(g), :] + stats_in[group(g), :]
            mask = valid(g)
            scales.append(
                (
                    (1.0 + label_weight) * mask / sums[:, 0:1],
                    mask / sums[:, 1:2],
                    label_weight * mask,
                    local_id(g),
                    group(g),
                )
            )
        for c in range(TILES):
            columns = slice(c * 128, (c + 1) * 128)
            parts = []
            for a, b, hot, emitted, rows in scales:
                value = a * expo[rows, columns] - b * post[rows, columns]
                parts.append(value - jnp.where(lanes == emitted - c * 128, hot, 0.0))
            dlog[pl.ds(pl.multiple_of(pair * 2 * FRAMES, 16), 2 * FRAMES), columns] = jnp.concatenate(parts, axis=0).astype(BF16)
        return carry

    for b in range(UTTS):
        stats_copies[b].wait_recv()
        lax.fori_loop(b * LABELS // 2, (b + 1) * LABELS // 2, dlog_step, 0, unroll=5)

    def ship(r, source, store, inbox, axis, rows, base):
        copies = []
        for d in distances(axis):
            start = base + around(axis, d) * rows
            codes, power = encode(source[r, pl.ds(pl.multiple_of(start, 16), rows), :])
            low = (d - 1) * (rows + 16)
            store[r, low : low + rows, :] = codes
            store[r, low + rows : low + rows + 16, :] = power
            place = slice(low, low + rows + 16)
            copies.append(send(store.at[r, place, :], inbox.at[r, place, :], device(axis, around(axis, d))))
        return copies

    def collect(r, copies, inbox, axis, rows, base):
        arrived(copies)
        place = pl.ds(pl.multiple_of(base + at[axis] * rows, 16), rows)
        total = term[r, place, :]
        for d in range(1, SIZE[axis]):
            low = (d - 1) * (rows + 16)
            total = total + decode(inbox[r, low : low + rows, :], inbox[r, low + rows : low + rows + 16, :])
        term[r, place, :] = total

    def sizes(r):
        first, middle, last = ORDERS[r]
        low = SIZE[first] * 16
        high = low * SIZE[middle]
        return low, high, at[last] * high, at[last] * high + at[middle] * low

    gathered = len(sent)
    third = {}

    def multiply(r):
        base = SLOT[r] * BLOCKS
        product = nn(hidden_t[base : base + BLOCKS, :], dlog[...])
        for c in range(TILES):
            term[r, pl.ds(c, BLOCKS, stride=16), :] = product[:, c * 128 : (c + 1) * 128]

    def depart(r):
        third[r] = ship(r, term, coded, coded_in, ORDERS[r][2], sizes(r)[1], 0)

    for r in (4, 0, 2):
        multiply(r)
        depart(r)

    act[...] = nt(dlog[...], weight[...]) * (1.0 - act[...] * act[...])
    side[...] = jnp.zeros_like(side)
    for b in range(UTTS):
        over_labels = jnp.zeros((FRAMES, JOINT), F32)
        for u in range(LABELS):
            start = (b * LABELS + u) * FRAMES
            part = act[start : start + FRAMES, :]
            over_labels += part
            row = b * SIDE + FRAMES + u
            side[row : row + 1, :] = jnp.sum(part, axis=0, keepdims=True)
        side[b * SIDE : b * SIDE + FRAMES, :] = over_labels
    theirs = side.at[pl.ds(pl.multiple_of((1 - core) * SIDE, 8), SIDE), :]
    pair_copy = send(theirs, pair_in, other_core)

    second, first_hop = {}, {}

    def turn(r):
        low, high, start, _ = sizes(r)
        collect(r, third[r], coded_in, ORDERS[r][2], high, 0)
        second[r] = ship(r, term, mid_coded, mid_in, ORDERS[r][1], low, start)

    def finish(low, high):
        axis = ORDERS[low][0]
        size, _, start, place = sizes(low)
        for r in range(low, high):
            collect(r, second[r], mid_in, ORDERS[r][1], size, start)
        first_hop[low] = []
        rows, base = (high - low) * 16, low * 24
        for d in distances(axis):
            spot_d = pl.ds(pl.multiple_of(place + around(axis, d) * 16, 16), 16)
            codes, power = encode(jnp.concatenate([term[r, spot_d, :] for r in range(low, high)], axis=0))
            last_code[d - 1, base : base + rows, :] = codes
            last_code[d - 1, base + rows : base + rows + 16, :] = power
            block = slice(base, base + rows + 16)
            first_hop[low].append(send(last_code.at[d - 1, block, :], last_in.at[d - 1, block, :], device(axis, around(axis, d))))

    for copy in sent[:gathered]:
        copy.wait_send()
    left[0] = gathered

    multiply(1)
    pair_copy.wait_recv()
    side_nat[...] = side[pl.ds(pl.multiple_of(core * SIDE, 8), SIDE), :] + pair_in[...]

    def fold(start, rows):
        strips = [side_nat[start : start + rows, k * 128 : (k + 1) * 128] for k in range(JOINT // 128)]
        if rows == FRAMES:
            strips.append(jnp.zeros((8, 128), F32))
        return jnp.concatenate(strips, axis=0)

    def code_side(slot):
        for start, rows, span, low in ((0, FRAMES, 128, 0), (FRAMES, SIDE - FRAMES, 80, 144)):
            codes, power = encode(fold(start, rows))
            side_code[slot, low : low + span, :] = codes
            side_code[slot, low + span : low + span + 16, :] = power

    def add_side(enc_ref, enc_count, pred_ref, pred_count):
        for ref, count, start, rows, span in ((enc_ref, enc_count, 0, FRAMES, 128), (pred_ref, pred_count, FRAMES, SIDE - FRAMES, 80)):
            total = decode(ref[0, 0:span, :], ref[0, span : span + 16, :])
            for d in range(1, count):
                total = total + decode(ref[d, 0:span, :], ref[d, span : span + 16, :])
            for k in range(JOINT // 128):
                side_nat[start : start + rows, k * 128 : (k + 1) * 128] += total[k * rows : (k + 1) * rows]

    code_side(0)
    enc_part, pred_part = side_code.at[0, 0:144, :], side_code.at[0, 144:240, :]
    y_copies = [send(enc_part, y_in.at[d - 1], device("y", around("y", d))) for d in distances("y")]
    x_copies = [send(pred_part, x_in.at[d - 1], device("x", around("x", d))) for d in distances("x")]

    depart(1)
    multiply(3)
    depart(3)

    for b in range(UTTS):
        for u in range(LABELS):
            g = b * LABELS + u
            rows = slice(g * FRAMES, (g + 1) * FRAMES)
            sums = stats[rows, :] + stats_in[rows, :]
            expsum, total, ent, cross, picked = (sums[:, k : k + 1] for k in range(5))
            lse = jnp.log(expsum)
            pair_loss = ent / total - jnp.log(total) - cross / total + lse + label_weight * (lse - picked)
            line = jnp.sum(jnp.where(lanes == rows_at, valid(g) * pair_loss, 0.0), axis=0, keepdims=True)
            loss_out[u, b : b + 1, :] = line[:, 0:FRAMES]

    turn(0)
    turn(2)

    arrived(y_copies + x_copies)
    add_side(y_in, 3, x_in, 3)
    code_side(1)
    z_low, z_high = at["z"] % 4, at["z"] // 4
    zh_copy = send(side_code.at[1, 0:144, :], zh_in.at[0], device("z", around("z", 4)))
    zl_copies = [
        send(side_code.at[1, 144:240, :], zl_in.at[d - 1], device("z", z_high * 4 + (z_low + d) % 4)) for d in range(1, 4)
    ]

    turn(4)
    turn(1)
    turn(3)
    finish(4, 5)

    finish(0, 2)
    finish(2, 4)

    def stacked(value):
        return jnp.concatenate([part.astype(F32) for part in split3(value)], axis=0).astype(BF16)

    def unstacked(value):
        rows = value.shape[0] // 3
        return value[0:rows] + value[rows : 2 * rows] + value[2 * rows : 3 * rows]

    arrived([zh_copy] + zl_copies)
    add_side(zh_in, 1, zl_in, 3)
    natural = unstacked(nt(stacked(side_nat[...]), perm[...]))
    grads[0:FRAMES, :] = unstacked(nt(stacked(natural[0:FRAMES]), enc_weight[...]))
    grads[FRAMES:SIDE, :] = unstacked(nt(stacked(natural[FRAMES:SIDE]), pred_weight[...]))
    grads_copy = send(grads, grads_in, other_core)

    for low, high in ((4, 5), (0, 2), (2, 4)):
        arrived(first_hop[low])
        rows, base = (high - low) * 16, low * 24
        total = jnp.concatenate(
            [term[r, pl.ds(pl.multiple_of(spot(r) * 16, 16), 16), :] for r in range(low, high)], axis=0
        )
        for d in distances(ORDERS[low][0]):
            total = total + decode(last_in[d - 1, base : base + rows, :], last_in[d - 1, base + rows : base + rows + 16, :])
        for r in range(low, high):
            result[r] = total[(r - low) * 16 : (r - low + 1) * 16]
            for c in range(TILES):
                grad_out[r : r + 1, c * 128 : (c + 1) * 128] = result[r, c : c + 1, :]

    grads_copy.wait_recv()
    enc_out[core] = grads[0:FRAMES, :]
    enc_out[1 - core] = grads_in[0:FRAMES, :]
    for u in range(LABELS):
        mine, other = grads[FRAMES + u : FRAMES + u + 1, :], grads_in[FRAMES + u : FRAMES + u + 1, :]
        pred_out[u, 0:1, :] = jnp.where(core == 0, mine, other)
        pred_out[u, 1:2, :] = jnp.where(core == 0, other, mine)

    drain()


def hand_over(*refs):
    half = len(refs) // 2
    for src, dst in zip(refs[:half], refs[half:]):
        dst[...] = src[...]


def per_device(
    enc_rows, pred_rows, enc_weight, pred_weight, out_weight, teacher, label_ids, frame_lengths, label_lengths
):
    vmem, anywhere = (pl.BlockSpec(memory_space=s) for s in (pltpu.VMEM, pl.ANY))
    scratch = [
        pltpu.SMEM((UTTS,), jnp.int32),
        pltpu.SMEM((UTTS,), jnp.int32),
        pltpu.SMEM((UTTS, LABELS), jnp.int32),
        pltpu.VMEM((UTTS, FRAMES, JOINT), BF16),
        pltpu.VMEM((LABELS, UTTS, JOINT), BF16),
        pltpu.VMEM((CHUNKS, VOCAB), BF16),
        pltpu.VMEM((CHUNKS, BLOCKS * 16, 128), BF16),
        pltpu.VMEM((JOINT, VOCAB), BF16),
        pltpu.VMEM((BLOCKS * 16, 128), F32),
        pltpu.VMEM((PADDED, JOINT), BF16),
        pltpu.VMEM((JOINT, PADDED), BF16),
        pltpu.VMEM((PADDED, JOINT), F32),
        pltpu.VMEM((PAIRS, VOCAB), F32),
        pltpu.VMEM((PAIRS, VOCAB), F32),
        pltpu.VMEM((PADDED, VOCAB), BF16),
        pltpu.VMEM((UTTS * LABELS, FRAMES, VOCAB), BF16),
        pltpu.VMEM((JOINT, JOINT), BF16),
        pltpu.VMEM((JOINT, JOINT), BF16),
        pltpu.VMEM((JOINT, JOINT), BF16),
        pltpu.VMEM((128, JOINT), F32),
        pltpu.VMEM((PAIRS, 128), F32),
        pltpu.VMEM((PAIRS, 128), F32),
        pltpu.VMEM((CHUNKS, BLOCKS * 16, 128), F32),
        pltpu.VMEM((CHUNKS, CODED, 128), jnp.int16),
        pltpu.VMEM((CHUNKS, CODED, 128), jnp.int16),
        pltpu.VMEM((CHUNKS, 3 * (128 + 16), 128), jnp.int16),
        pltpu.VMEM((CHUNKS, 3 * (128 + 16), 128), jnp.int16),
        pltpu.VMEM((7, 128, 128), jnp.int16),
        pltpu.VMEM((7, 128, 128), jnp.int16),
        pltpu.VMEM((2 * SIDE, JOINT), F32),
        pltpu.VMEM((2, 240, 128), jnp.int16),
        pltpu.VMEM((SIDE, JOINT), F32),
        pltpu.VMEM((3, 144, 128), jnp.int16),
        pltpu.VMEM((3, 96, 128), jnp.int16),
        pltpu.VMEM((1, 144, 128), jnp.int16),
        pltpu.VMEM((3, 96, 128), jnp.int16),
        pltpu.VMEM((SIDE, JOINT), F32),
        pltpu.VMEM((SIDE, JOINT), F32),
        pltpu.VMEM((SIDE, JOINT), F32),
        pltpu.VMEM((CHUNKS, 16, 128), F32),
        pltpu.SemaphoreType.DMA((9,)),
        pltpu.SemaphoreType.DMA((144,)),
        pltpu.SemaphoreType.DMA((144,)),
    ]
    shapes = (
        jax.ShapeDtypeStruct((LABELS, UTTS, FRAMES), F32),
        jax.ShapeDtypeStruct((UTTS, FRAMES, JOINT), F32),
        jax.ShapeDtypeStruct((LABELS, UTTS, JOINT), F32),
        jax.ShapeDtypeStruct((CHUNKS, VOCAB), F32),
    )
    results = pl.pallas_call(
        kernel,
        out_shape=shapes,
        in_specs=[anywhere] * 9,
        out_specs=(vmem,) * 4,
        scratch_shapes=scratch,
        compiler_params=pltpu.CompilerParams(
            collective_id=0, has_side_effects=True, vmem_limit_bytes=56 * 1024 * 1024
        ),
    )(
        frame_lengths, label_lengths, label_ids, enc_rows, pred_rows.transpose(1, 0, 2), out_weight,
        enc_weight, pred_weight, teacher.transpose(0, 2, 1, 3).reshape(UTTS * LABELS, FRAMES, VOCAB),
    )
    loss, grad_enc, grad_pred, grad_out = pl.pallas_call(
        hand_over, out_shape=shapes, in_specs=[vmem] * 4, out_specs=(vmem,) * 4
    )(*results)
    return loss.transpose(1, 2, 0), grad_enc, grad_pred.transpose(1, 0, 2), grad_out


def solution(mesh):
    return jax.shard_map(
        per_device,
        mesh=mesh,
        in_specs=(
            P(None, "tm", None),
            P(None, "label", None),
            P(),
            P(),
            P(("tm", "label"), "vocab"),
            P(None, "tm", "label", "vocab"),
            P(None, "label"),
            P(),
            P(),
        ),
        out_specs=(
            P(None, "tm", "label"),
            P(None, "tm", None),
            P(None, "label", None),
            P(("tm", "label"), "vocab"),
        ),
        check_vma=False,
    )
```
